32 devices in a mesh: groups: 2 (over y), dev: 16 (over z, x, core).
Axes of the slice: x: 2, y: 2, z: 4, core: 2. Of those that a mesh axis runs over, the one named last changes fastest.
Arguments:
- volumes: bfloat16 [256, 262144], P(('groups', 'dev')), parts along dimension 0, may hold values from -6 to 6
- rotations: bfloat16 [3, 1024, 1024], replicated, may hold values from -0.1875 to 0.1875
- turn_ids: int32 [256], P(('groups', 'dev')), parts along dimension 0, may hold values from 0 to 2
- shifts: int32 [256, 3], P(('groups', 'dev')), parts along dimension 0, may hold values from -4 to 4
- defocus: float32 [256], P(('groups', 'dev')), parts along dimension 0, may hold values from 0.05 to 0.5
- labels: int32 [256], P(('groups', 'dev')), parts along dimension 0, may hold values from 0 to 47
- references: bfloat16 [96, 65536], P('groups', 'dev'), parts along dimension 0, may hold values from -6 to 6
Outputs:
- new_refs: float32 [96, 65536], P('groups', 'dev'), parts along dimension 0
- scores: float32 [256], P(('groups', 'dev')), parts along dimension 0
The draws below stay inside these ranges and needn't reach their ends.
There are 2 independent parts, one for each index of `groups`. The reference program is written for one: setup_inputs(seed, part) draws one part's arguments, and reference() takes and returns one part's arrays. A program takes and returns all parts, laid end to end along the dimension named above; an argument that names none is the same for every part. Nothing has to cross between parts.
All inputs are finite; a program needn't handle non-finite values.
Results may differ from the reference program's by a relative error of at most 0.0069.
Values may be sent and summed in bfloat16 or wider, within the bound.
A program may use at most 128 MiB of HBM per device.

```python
import math
import jax
import jax.numpy as jnp
from jax import lax

BOX = 64
BAND = 32
CLASSES = 48
NROT = 3
SHIFT_MAX = 4
PARTICLES = 128


def plant(entries, own_key, smallest, high):
    extent = entries.shape
    index_at = [jax.random.randint(jax.random.fold_in(own_key, axis), (), 0, extent[axis]) for axis in range(len(extent))]
    entries = entries.at[tuple(index_at)].set(smallest)
    longest = extent.index(max(extent))
    index_at[longest] = (index_at[longest] + 1) % extent[longest]
    return entries.at[tuple(index_at)].set(high)


def shard_levels(own_key, extent, cuts, least, high):
    gain, own = 1.0, jax.random.fold_in(own_key, 6)
    for dim, parts in cuts:
        steps = jnp.exp(jax.random.uniform(jax.random.fold_in(own, dim), (parts,), jnp.float32, least / len(cuts), high / len(cuts)))
        gain = gain * jnp.repeat(steps, extent[dim] // parts).reshape([-1 if axis == dim else 1 for axis in range(len(extent))])
    return gain


def centred(own_key, shape, spread, bound, shards=(), kind=jnp.bfloat16):
    drawn = jax.random.normal(own_key, shape, jnp.float32) * spread
    if len(shards) > 0:
        drawn = shard_levels(own_key, shape, shards, -0.22, 0.18) * drawn
    return jnp.clip(drawn, min=-bound, max=bound).astype(kind)


def setup_inputs(seed: int = 0, part: int = 0) -> dict:
    key_of = jax.random.split(jax.random.key(seed), 8)
    own_keys = jax.random.split(jax.random.fold_in(key_of[7], part), 8)
    return {
        "volumes": centred(own_keys[0], (PARTICLES, BOX ** 3), 1.0, 6.0, ((0, 16),)),
        "rotations": centred(key_of[1], (NROT, BAND * BAND, BAND * BAND), (BAND * BAND) ** -0.5, 0.1875),
        "turn_ids": plant(jax.random.randint(own_keys[2], (PARTICLES,), 0, NROT), jax.random.fold_in(own_keys[2], 1), 0, NROT - 1).astype(jnp.int32),
        "shifts": plant(jax.random.randint(own_keys[3], (PARTICLES, 3), -SHIFT_MAX, SHIFT_MAX + 1), jax.random.fold_in(own_keys[3], 1), -SHIFT_MAX, SHIFT_MAX).astype(jnp.int32),
        "defocus": jnp.clip(jnp.exp(math.log(0.5) - 2.3025851 * jax.random.uniform(own_keys[4], (PARTICLES,), jnp.float32) ** shard_levels(own_keys[4], (PARTICLES,), ((0, 16),), -0.2, 0.2)), 0.05, 0.5),
        "labels": plant(jax.random.randint(own_keys[5], (PARTICLES,), 0, CLASSES), jax.random.fold_in(own_keys[5], 1), 0, CLASSES - 1).astype(jnp.int32),
        "references": centred(own_keys[6], (CLASSES, 2 * BAND ** 3), 1.0, 6.0, ((1, 16),)),
    }


TWO_PI = 2.0 * math.pi

def dft_tables():
    sample = jnp.arange(BOX, dtype=jnp.int32)
    frequency = jnp.arange(BAND, dtype=jnp.int32) - BAND // 2
    phase_index = jnp.mod(sample[:, None] * frequency[None, :], BOX).astype(jnp.float32)
    phase_angle = phase_index * (TWO_PI / BOX)
    norm_scale = 1.0 / math.sqrt(BOX)
    cosine = (jnp.cos(phase_angle) * norm_scale).astype(jnp.bfloat16)
    sine_part = (jnp.sin(phase_angle) * norm_scale).astype(jnp.bfloat16)
    first_table = jnp.concatenate([cosine, -sine_part], axis=1)
    mixing = jnp.stack([jnp.stack([cosine, sine_part]), jnp.stack([-sine_part, cosine])])
    return (first_table, mixing)

def transform(volumes):
    particle_count = volumes.shape[0]
    first_table, mixing = dft_tables()
    section_z = jnp.dot(volumes.reshape(-1, BOX), first_table, preferred_element_type=jnp.float32)
    section_z = section_z.astype(jnp.bfloat16).reshape(particle_count, BOX, BOX, 2, BAND)
    section_y = jnp.einsum('pxybz,abyj->pxjaz', section_z.astype(jnp.float32), mixing.astype(jnp.float32), precision=lax.Precision.HIGHEST).astype(jnp.bfloat16)
    section_x = jnp.einsum('pxkbz,abxj->pjkaz', section_y.astype(jnp.float32), mixing.astype(jnp.float32), precision=lax.Precision.HIGHEST).astype(jnp.bfloat16)
    return section_x.reshape(particle_count, BAND * BAND, 2 * BAND)

def band_grid(start_cell, cell_count):
    cell_index = start_cell + jnp.arange(cell_count, dtype=jnp.int32)
    freq_x = cell_index // BAND - BAND // 2
    freq_y = cell_index % BAND - BAND // 2
    freq_z = jnp.arange(BAND, dtype=jnp.int32) - BAND // 2
    return (freq_x[:, None], freq_y[:, None], freq_z[None, :])

def contrast(defocus, freq_x, freq_y, freq_z):
    radius = (freq_x * freq_x + freq_y * freq_y + freq_z * freq_z).astype(jnp.float32)
    return jnp.sin(defocus[:, None, None] * radius[None] / BAND + 0.3)

def weigh_spectra(spectrum, turn_ids, shifts, defocus, rotations):
    particle_count = spectrum.shape[0]
    taken = rotations[turn_ids]
    turned = jnp.einsum('pmn,pnc->pmc', taken.astype(jnp.float32), spectrum.astype(jnp.float32), precision=lax.Precision.HIGHEST)
    freq_x, freq_y, freq_z = band_grid(0, BAND * BAND)
    shift_dot = freq_x[None] * shifts[:, 0, None, None] + freq_y[None] * shifts[:, 1, None, None] + freq_z[None] * shifts[:, 2, None, None]
    phase_angle = jnp.mod(shift_dot, BOX).astype(jnp.float32) * (TWO_PI / BOX)
    cosine = jnp.cos(phase_angle)
    sine_part = jnp.sin(phase_angle)
    real_part = turned[:, :, :BAND]
    imag_part = turned[:, :, BAND:]
    weight = contrast(defocus, freq_x, freq_y, freq_z)
    aligned = jnp.concatenate([weight * (real_part * cosine - imag_part * sine_part), weight * (real_part * sine_part + imag_part * cosine)], axis=2)
    return (aligned.astype(jnp.bfloat16).reshape(particle_count, -1), (weight * weight).reshape(particle_count, -1))

def wiener(class_sum, weight_sum):
    class_count, column_count = class_sum.shape
    cell_count = weight_sum.shape[1] // BAND
    filtered = class_sum.reshape(class_count, cell_count, 2, BAND) / (weight_sum.reshape(class_count, cell_count, 1, BAND) + 1.0)
    return filtered.reshape(class_count, column_count)

def reference(volumes, rotations, turn_ids, shifts, defocus, labels, references):
    per_block = 8
    block_count = PARTICLES // per_block

    def one_block(inputs_block):
        volume_rows, turn_block, shift_block, focus_block = inputs_block
        spectrum = transform(volume_rows)
        return weigh_spectra(spectrum, turn_block, shift_block, focus_block, rotations)
    aligned, squared = lax.map(one_block, (volumes.reshape(block_count, per_block, -1), turn_ids.reshape(block_count, per_block), shifts.reshape(block_count, per_block, 3), defocus.reshape(block_count, per_block)))
    aligned = aligned.reshape(PARTICLES, -1)
    squared = squared.reshape(PARTICLES, -1)
    member = labels[:, None] == jnp.arange(CLASSES, dtype=jnp.int32)[None, :]
    class_sum = jnp.dot(member.astype(jnp.bfloat16).T, aligned, preferred_element_type=jnp.float32)
    weight_sum = jnp.dot(member.astype(jnp.float32).T, squared, preferred_element_type=jnp.float32, precision=lax.Precision.HIGHEST)
    new_refs = wiener(class_sum, weight_sum)
    chosen = references[labels]
    agreement = lax.optimization_barrier(jnp.sum(aligned.astype(jnp.float32) * chosen.astype(jnp.float32), axis=1))
    energy = lax.optimization_barrier(jnp.sum(jnp.square(aligned.astype(jnp.float32)), axis=1))
    scores = agreement / jnp.sqrt(energy + 1e-06)
    return (new_refs, scores)
```

```python
import math

import jax
import jax.numpy as jnp
from jax import lax
from jax.sharding import PartitionSpec as P

BOX = 64
BAND = 32


TWO_PI = 2.0 * math.pi


def dft_tables():
    sample = jnp.arange(BOX, dtype=jnp.int32)
    frequency = jnp.arange(BAND, dtype=jnp.int32) - BAND // 2
    phase_index = jnp.mod(sample[:, None] * frequency[None, :], BOX).astype(jnp.float32)
    phase_angle = phase_index * (TWO_PI / BOX)
    norm_scale = 1.0 / math.sqrt(BOX)
    cosine = (jnp.cos(phase_angle) * norm_scale).astype(jnp.bfloat16)
    sine_part = (jnp.sin(phase_angle) * norm_scale).astype(jnp.bfloat16)
    first_table = jnp.concatenate([cosine, -sine_part], axis=1)
    mixing = jnp.stack([jnp.stack([cosine, sine_part]), jnp.stack([-sine_part, cosine])])
    return (first_table, mixing)


def transform(volumes):
    particle_count = volumes.shape[0]
    first_table, mixing = dft_tables()
    section_z = jnp.dot(volumes.reshape(-1, BOX), first_table, preferred_element_type=jnp.float32)
    section_z = section_z.astype(jnp.bfloat16).reshape(particle_count, BOX, BOX, 2, BAND)
    section_y = jnp.einsum(
        "pxybz,abyj->pxjaz", section_z, mixing, preferred_element_type=jnp.float32
    ).astype(jnp.bfloat16)
    section_x = jnp.einsum(
        "pxkbz,abxj->pjkaz", section_y, mixing, preferred_element_type=jnp.float32
    ).astype(jnp.bfloat16)
    return section_x.reshape(particle_count, BAND * BAND, 2 * BAND)


def band_grid(cell_count, first_cell=0):
    cell_index = first_cell + jnp.arange(cell_count, dtype=jnp.int32)
    freq_x = cell_index // BAND - BAND // 2
    freq_y = cell_index % BAND - BAND // 2
    freq_z = jnp.arange(BAND, dtype=jnp.int32) - BAND // 2
    return (freq_x[:, None], freq_y[:, None], freq_z[None, :])


def contrast(defocus, freq_x, freq_y, freq_z):
    radius = (freq_x * freq_x + freq_y * freq_y + freq_z * freq_z).astype(jnp.float32)
    return jnp.sin(defocus[:, None, None] * radius[None] / BAND + 0.3)


def weigh_spectra(spectrum, turn_ids, shifts, defocus, rotations):
    particle_count = spectrum.shape[0]
    taken = rotations[turn_ids]
    turned = jnp.einsum("pmn,pnc->pmc", taken, spectrum, preferred_element_type=jnp.float32)
    freq_x, freq_y, freq_z = band_grid(BAND * BAND)
    shift_dot = (
        freq_x[None] * shifts[:, 0, None, None]
        + freq_y[None] * shifts[:, 1, None, None]
        + freq_z[None] * shifts[:, 2, None, None]
    )
    phase_angle = jnp.mod(shift_dot, BOX).astype(jnp.float32) * (TWO_PI / BOX)
    cosine = jnp.cos(phase_angle)
    sine_part = jnp.sin(phase_angle)
    real_part = turned[:, :, :BAND]
    imag_part = turned[:, :, BAND:]
    weight = contrast(defocus, freq_x, freq_y, freq_z)
    aligned = jnp.concatenate(
        [
            weight * (real_part * cosine - imag_part * sine_part),
            weight * (real_part * sine_part + imag_part * cosine),
        ],
        axis=2,
    )
    return aligned.astype(jnp.bfloat16).reshape(particle_count, -1)


def wiener(class_sum, weight_sum):
    class_count, column_count = class_sum.shape
    cell_count = weight_sum.shape[1] // BAND
    filtered = class_sum.reshape(class_count, cell_count, 2, BAND) / (
        weight_sum.reshape(class_count, cell_count, 1, BAND) + 1.0
    )
    return filtered.reshape(class_count, column_count)


def on_device(volumes, rotations, turn_ids, shifts, defocus, labels, references):
    class_count, column_count = references.shape
    cell_count = column_count // (2 * BAND)
    spectrum = transform(volumes)
    aligned = weigh_spectra(spectrum, turn_ids, shifts, defocus, rotations)
    wide_rows = aligned.astype(jnp.float32)
    energy = jnp.sum(wide_rows * wide_rows, axis=1)
    facts = jnp.stack([labels.astype(jnp.float32), defocus])
    facts = lax.all_gather(facts, "dev", axis=1, tiled=True)
    held = lax.all_to_all(aligned, "dev", split_axis=1, concat_axis=0, tiled=True)
    member = facts[0][:, None] == jnp.arange(class_count, dtype=jnp.float32)[None, :]
    table = member.astype(jnp.bfloat16)
    freq_x, freq_y, freq_z = band_grid(cell_count, lax.axis_index("dev") * cell_count)
    weight = contrast(facts[1], freq_x, freq_y, freq_z)
    squared = (weight * weight).reshape(facts.shape[1], -1)
    class_sum = jnp.dot(table.T, held, preferred_element_type=jnp.float32)
    weight_sum = jnp.dot(
        member.astype(jnp.float32).T,
        squared,
        preferred_element_type=jnp.float32,
        precision=lax.Precision.HIGHEST,
    )
    chosen = jnp.dot(table, references, preferred_element_type=jnp.float32)
    part = jnp.sum(held.astype(jnp.float32) * chosen, axis=1)
    agreement = lax.psum_scatter(part, "dev", scatter_dimension=0, tiled=True)
    scores = agreement / jnp.sqrt(energy + 1e-06)
    return (wiener(class_sum, weight_sum), scores)


def solution(mesh):
    return jax.shard_map(
        on_device,
        mesh=mesh,
        in_specs=(
            P(("groups", "dev"), None),
            P(),
            P(("groups", "dev")),
            P(("groups", "dev"), None),
            P(("groups", "dev")),
            P(("groups", "dev")),
            P("groups", "dev"),
        ),
        out_specs=(P("groups", "dev"), P(("groups", "dev"))),
        check_vma=False,
    )
```

```python
import math

import jax
import jax.numpy as jnp
import ml_dtypes
import numpy as np
from jax import lax
from jax.experimental import pallas as pl
from jax.experimental.pallas import tpu as pltpu
from jax.sharding import PartitionSpec as P

BOX = 64
BAND = 32
ROWS = 8
CELLS = BAND * BAND
LANES = 128
TWO_PI = 2.0 * math.pi
VMEM = pl.BlockSpec(memory_space=pltpu.VMEM)
SMEM = pl.BlockSpec(memory_space=pltpu.SMEM)
F32 = jnp.float32
BF16 = jnp.bfloat16


def rounded(table):
    return np.asarray(table, np.float32).astype(ml_dtypes.bfloat16)


def tables():
    n = np.arange(BOX)
    k = np.arange(BAND) - BAND // 2
    angle = TWO_PI * ((n[:, None] * k[None, :]) % BOX) / BOX
    cosine, sine = np.cos(angle) / 8.0, np.sin(angle) / 8.0
    by_z = np.zeros((4, 64, 2, 4, 32))
    for y in range(4):
        by_z[y, :, 0, y] = cosine
        by_z[y, :, 1, y] = -sine
    mixing = np.array([[cosine, sine], [-sine, cosine]])
    by_x = np.zeros((8, 2, 2, 16, 2, 64, 8))
    for p in range(8):
        by_x[p, :, :, :, :, :, p] = mixing.reshape(2, 2, 64, 2, 16).transpose(3, 0, 4, 1, 2)
    q = np.arange(16)
    turn = TWO_PI * ((q[:, None] * q[None, :]) % 16) / 16
    c, s = np.cos(turn) / 4.0, np.sin(turn) / 4.0
    by_h = np.zeros((16, 2, 16, 16, 2, 16))
    for low in range(16):
        by_h[:, 0, low, :, 0, low] = c
        by_h[:, 0, low, :, 1, low] = s
        by_h[:, 1, low, :, 0, low] = -s
        by_h[:, 1, low, :, 1, low] = c
    by_y = np.zeros((16, 2, 4, 32, 2, 2, 2, 32))
    for high in range(2):
        for y in range(4):
            part = TWO_PI * (((high * 16 + q - 16) * y) % 64) / 64
            c, s = (np.cos(part) / 2.0)[:, None], (np.sin(part) / 2.0)[:, None]
            z = np.arange(32)
            by_y[:, 0, y, z, high, 0, 0, z] = c
            by_y[:, 1, y, z, high, 0, 0, z] = s
            by_y[:, 0, y, z, high, 0, 1, z] = -s
            by_y[:, 1, y, z, high, 0, 1, z] = c
            by_y[:, 0, y, z, high, 1, 0, z] = s
            by_y[:, 1, y, z, high, 1, 0, z] = -c
            by_y[:, 0, y, z, high, 1, 1, z] = c
            by_y[:, 1, y, z, high, 1, 1, z] = s
    return (
        rounded(by_z.reshape(256, 256)),
        rounded(by_x.reshape(512, 1024)),
        rounded(by_h.reshape(512, 512)),
        rounded(by_y.reshape(16, 256, 256)),
    )


def dot(a, b):
    return jnp.dot(a, b, preferred_element_type=F32)


def root(count):
    angle = (count - 64.0 * jnp.floor(count / 64.0)) * (TWO_PI / 64.0)
    return jnp.cos(angle), jnp.sin(angle)


def halves(x):
    high = x.astype(BF16).astype(F32)
    return high, x - high


def factors(facts):
    defocus, sx, sy, sz = (facts[:, i : i + 1] for i in range(1, 5))
    cell = lax.broadcasted_iota(jnp.int32, (ROWS, CELLS), 1)
    kx = (cell // BAND - BAND // 2).astype(F32)
    ky = (cell % BAND - BAND // 2).astype(F32)
    focus = defocus * (kx * kx + ky * ky) / BAND + 0.3
    cos_a, sin_a = root(kx * sx + ky * sy)
    cos_f, sin_f = jnp.cos(focus), jnp.sin(focus)
    rows = [halves(x) for x in (sin_f * cos_a, sin_f * sin_a, cos_f * cos_a, cos_f * sin_a)]
    lane = lax.broadcasted_iota(jnp.int32, (ROWS, LANES), 1)
    kz = (lane % BAND - BAND // 2).astype(F32)
    cos_b, sin_b = root(kz * sz)
    first = lane < LANES // 2
    one = jnp.where(first, cos_b, sin_b)
    two = jnp.where(first, -sin_b, cos_b)
    focus = defocus * (kz * kz) / BAND
    cos_f, sin_f = jnp.cos(focus), jnp.sin(focus)
    lanes = [halves(x) for x in (cos_f * one, cos_f * two, sin_f * one, sin_f * two)]
    blank = jnp.zeros((32, CELLS), F32)
    left = jnp.concatenate(
        [r[0] for r in rows] + [r[0] for r in rows] + [r[1] for r in rows] + [blank], axis=0
    )
    right = jnp.concatenate(
        [x[0] for x in lanes] + [x[1] for x in lanes] + [x[0] for x in lanes] + [blank[:, :LANES]], axis=0
    )
    owner = lax.broadcasted_iota(jnp.int32, (LANES, LANES), 0) % ROWS
    right = [jnp.where(owner == p, right, 0.0) for p in range(ROWS)]
    return left.T.astype(BF16), jnp.concatenate(right, axis=1).astype(BF16)


def spectra(turn_ref, vol_ref, rot_ref, facts_ref, z_ref, x_ref, h_ref, y_ref,
            out_ref, energy_ref, by_z, by_x, by_h, spec, left_ref, right_ref, wide):
    owners, _, pairs, _ = out_ref.shape
    left, right = factors(facts_ref[...])
    left_ref[...] = left
    right_ref[...] = right

    @pl.loop(0, 16)
    def _(h):
        got = dot(vol_ref[:, pl.ds(pl.multiple_of(h * 256, 256), 256)], z_ref[...]).astype(BF16)
        at = pl.ds(pl.multiple_of(h * 128, 128), 128)
        by_z[0:512, at] = got[:, :128]
        by_z[512:1024, at] = got[:, 128:]

    @pl.loop(0, 8)
    def _(h2):
        got = dot(x_ref[...], by_z[:, pl.ds(pl.multiple_of(h2 * 256, 256), 256)]).astype(BF16)
        for i in range(2):
            to = pl.ds(pl.multiple_of(h2 * 64 + i * 32, 32), 32)
            for g in range(16):
                by_x[to, g * 128 : (g + 1) * 128] = got[g * 32 : (g + 1) * 32, i * 128 : (i + 1) * 128]

    @pl.loop(0, 8)
    def _(g2):
        got = dot(h_ref[...], by_x[:, pl.ds(pl.multiple_of(g2 * 256, 256), 256)]).astype(BF16)
        got = got.reshape(16, 2, 16, 256)
        for i in range(2):
            to = pl.ds(pl.multiple_of(g2 * 32 + i * 16, 16), 16)
            for c in range(2):
                by_h[:, to, c * 128 : (c + 1) * 128] = got[:, c, :, i * 128 : (i + 1) * 128]

    @pl.loop(0, 16)
    def _(q):
        got = dot(by_h[q], y_ref[q])
        for high in range(2):
            spec[pl.ds(high * 16 + q, 256, stride=32), :] = got[:, high * 128 : (high + 1) * 128]

    first = lax.broadcasted_iota(jnp.int32, (CELLS // 2, LANES), 1) < LANES // 2

    @pl.loop(0, ROWS)
    def _(p):
        own = spec[pl.ds(pl.multiple_of(p * CELLS, CELLS), CELLS), :].astype(BF16)
        turned = dot(rot_ref[turn_ref[p]], own)
        factor = dot(left_ref[...], right_ref[:, pl.ds(pl.multiple_of(p * 128, 128), 128)])
        both = turned * factor
        wide[...] = both + pltpu.roll(both, LANES // 2, 1)
        packed = jnp.where(first, wide[pl.ds(0, CELLS // 2, stride=2), :], wide[pl.ds(1, CELLS // 2, stride=2), :])
        packed = packed.astype(BF16)
        out_ref[:, p] = packed.reshape(owners, pairs, LANES)
        long = packed.astype(F32)
        energy_ref[pl.ds(p, 1), :] = jnp.sum(long * long, axis=0, keepdims=True)


def classes(owners, send_ref, facts_ref, energy_ref, refs_ref, new_ref, score_ref,
            held, facts, wide, chosen, below, parts, answer, sems):
    me = lax.axis_index("dev")
    class_count, columns = refs_ref.shape
    pairs = columns // LANES
    particles = owners * ROWS

    def copy(i, k):
        to = lax.rem(me + k, owners)
        src = (facts_ref, send_ref.at[to], parts.at[to])[i]
        dst = (facts, held, answer)[i]
        return pltpu.make_async_remote_copy(
            src_ref=src, dst_ref=dst.at[me],
            send_sem=sems.at[2 * i, k], recv_sem=sems.at[2 * i + 1, k],
            device_id={"dev": to}, device_id_type=pl.DeviceIdType.MESH,
        )

    barrier = pltpu.get_barrier_semaphore()

    @pl.loop(1, owners)
    def _(k):
        pl.semaphore_signal(
            barrier, inc=1, device_id={"dev": lax.rem(me + k, owners)}, device_id_type=pl.DeviceIdType.MESH
        )

    pl.semaphore_wait(barrier, owners - 1)

    @pl.loop(1, owners)
    def _(k):
        copy(0, k).start()

    @pl.loop(1, owners)
    def _(k):
        copy(1, k).start()

    facts[me] = facts_ref[...]
    held[me] = send_ref[me]

    @pl.loop(1, owners)
    def _(k):
        copy(0, k).wait()

    known = facts[...].reshape(particles, LANES)
    lane = lax.broadcasted_iota(jnp.int32, (particles, LANES), 1)
    member = jnp.where(known[:, 0:1] == lane.astype(F32), 1.0, 0.0)
    across = member.T[:class_count]
    defocus = known[:, 1:2]
    one = lax.broadcasted_iota(jnp.int32, (1, LANES), 1)
    kz = one % BAND - BAND // 2

    @pl.loop(0, pairs)
    def _(r):
        cell = (me * pairs + r) * 2 + one // (2 * BAND)
        kx = cell // BAND - BAND // 2
        ky = cell % BAND - BAND // 2
        radius = (kx * kx + ky * ky + kz * kz).astype(F32)
        weight = jnp.sin(defocus * radius / BAND + 0.3)
        total = jnp.dot(across, weight * weight, preferred_element_type=F32, precision=lax.Precision.HIGHEST)
        below[r] = 1.0 / (total + 1.0)
        at = pl.ds(pl.multiple_of(r * LANES, LANES), LANES)
        chosen[r] = dot(member[:, :class_count].astype(BF16), refs_ref[:, at])

    @pl.loop(1, owners)
    def _(k):
        copy(1, k).wait()

    wide[...] = held[...].astype(F32).reshape(particles * pairs, LANES)
    parts[...] = jnp.zeros_like(parts)

    @pl.loop(0, pairs)
    def _(r):
        rows = wide[pl.ds(r, particles, stride=pairs), :]
        total = dot(across.astype(BF16), rows.astype(BF16))
        new_ref[:, pl.ds(pl.multiple_of(r * LANES, LANES), LANES)] = total * below[r]
        parts[...] += (rows * chosen[r]).reshape(owners, ROWS, LANES)

    @pl.loop(1, owners)
    def _(k):
        copy(2, k).start()

    answer[me] = parts[me]

    @pl.loop(1, owners)
    def _(k):
        copy(2, k).wait()

    agreement = jnp.sum(jnp.sum(answer[...], axis=0), axis=1, keepdims=True)
    energy = jnp.sum(energy_ref[...], axis=1, keepdims=True)
    score_ref[...] = jnp.broadcast_to(agreement / jnp.sqrt(energy + 1e-06), (ROWS, LANES))


def on_device(owners, volumes, rotations, turn_ids, shifts, defocus, labels, references):
    class_count, columns = references.shape
    pairs = columns // LANES
    particles = owners * ROWS
    facts = jnp.concatenate(
        [labels.astype(F32)[:, None], defocus[:, None], shifts.astype(F32), jnp.zeros((ROWS, LANES - 5), F32)], axis=1
    )
    rows = volumes.reshape(ROWS, BOX, BOX * BOX).transpose(1, 0, 2).reshape(BOX * ROWS, BOX * BOX)
    send, energy = pl.pallas_call(
        spectra,
        out_shape=(
            jax.ShapeDtypeStruct((owners, ROWS, pairs, LANES), BF16),
            jax.ShapeDtypeStruct((ROWS, LANES), F32),
        ),
        in_specs=[SMEM] + [VMEM] * 7,
        out_specs=(VMEM, VMEM),
        scratch_shapes=[
            pltpu.VMEM((1024, 2048), BF16),
            pltpu.VMEM((512, 2048), BF16),
            pltpu.VMEM((16, 256, 256), BF16),
            pltpu.VMEM((ROWS * CELLS, LANES), F32),
            pltpu.VMEM((CELLS, LANES), BF16),
            pltpu.VMEM((LANES, ROWS * LANES), BF16),
            pltpu.VMEM((CELLS, LANES), F32),
        ],
        compiler_params=pltpu.CompilerParams(vmem_limit_bytes=48 * 1024 * 1024),
    )(turn_ids, rows, rotations, facts, *(jnp.asarray(t) for t in tables()))
    new_refs, scores = pl.pallas_call(
        lambda *refs: classes(owners, *refs),
        out_shape=(
            jax.ShapeDtypeStruct((class_count, columns), F32),
            jax.ShapeDtypeStruct((ROWS, LANES), F32),
        ),
        in_specs=[VMEM] * 4,
        out_specs=(VMEM, VMEM),
        scratch_shapes=[
            pltpu.VMEM((owners, ROWS, pairs, LANES), BF16),
            pltpu.VMEM((owners, ROWS, LANES), F32),
            pltpu.VMEM((particles * pairs, LANES), F32),
            pltpu.VMEM((pairs, particles, LANES), F32),
            pltpu.VMEM((pairs, class_count, LANES), F32),
            pltpu.VMEM((owners, ROWS, LANES), F32),
            pltpu.VMEM((owners, ROWS, LANES), F32),
            pltpu.SemaphoreType.DMA((6, owners)),
        ],
        compiler_params=pltpu.CompilerParams(
            collective_id=0, has_side_effects=True, vmem_limit_bytes=48 * 1024 * 1024
        ),
    )(send, facts, energy, references)
    return new_refs, scores[:, 0]


def solution(mesh):
    owners = mesh.shape["dev"]
    return jax.shard_map(
        lambda *args: on_device(owners, *args),
        mesh=mesh,
        in_specs=(
            P(("groups", "dev"), None),
            P(),
            P(("groups", "dev")),
            P(("groups", "dev"), None),
            P(("groups", "dev")),
            P(("groups", "dev")),
            P("groups", "dev"),
        ),
        out_specs=(P("groups", "dev"), P(("groups", "dev"))),
        check_vma=False,
    )
```

```python
import math

import jax
import jax.numpy as jnp
import ml_dtypes
import numpy as np
from jax import lax
from jax.experimental import pallas as pl
from jax.experimental.pallas import tpu as pltpu
from jax.sharding import PartitionSpec as P

BOX = 64
BAND = 32
ROWS = 8
CELLS = BAND * BAND
LANES = 128
CHUNKS = 4
GROUP = 2
TWO_PI = 2.0 * math.pi
VMEM = pl.BlockSpec(memory_space=pltpu.VMEM)
HBM = pl.BlockSpec(memory_space=pltpu.HBM)
SMEM = pl.BlockSpec(memory_space=pltpu.SMEM)
F32 = jnp.float32
BF16 = jnp.bfloat16


def rounded(table):
    return np.asarray(table, np.float32).astype(ml_dtypes.bfloat16)


def tables():
    n = np.arange(BOX)
    k = np.arange(BAND) - BAND // 2
    angle = TWO_PI * ((n[:, None] * k[None, :]) % BOX) / BOX
    cosine, sine = np.cos(angle) / 8.0, np.sin(angle) / 8.0
    by_z = np.zeros((4, 64, 2, 4, 32))
    for y in range(4):
        by_z[y, :, 0, y] = cosine
        by_z[y, :, 1, y] = -sine
    mixing = np.array([[cosine, sine], [-sine, cosine]])
    by_x = np.zeros((8, 2, 2, 16, 2, 64, 8))
    for p in range(8):
        by_x[p, :, :, :, :, :, p] = mixing.reshape(2, 2, 64, 2, 16).transpose(3, 0, 4, 1, 2)
    q = np.arange(16)
    turn = TWO_PI * ((q[:, None] * q[None, :]) % 16) / 16
    c, s = np.cos(turn) / 4.0, np.sin(turn) / 4.0
    by_h = np.zeros((16, 2, 16, 16, 2, 16))
    for low in range(16):
        by_h[:, 0, low, :, 0, low] = c
        by_h[:, 0, low, :, 1, low] = s
        by_h[:, 1, low, :, 0, low] = -s
        by_h[:, 1, low, :, 1, low] = c
    by_y = np.zeros((16, 2, 4, 32, 2, 2, 2, 32))
    for high in range(2):
        for y in range(4):
            part = TWO_PI * (((high * 16 + q - 16) * y) % 64) / 64
            c, s = (np.cos(part) / 2.0)[:, None], (np.sin(part) / 2.0)[:, None]
            z = np.arange(32)
            by_y[:, 0, y, z, high, 0, 0, z] = c
            by_y[:, 1, y, z, high, 0, 0, z] = s
            by_y[:, 0, y, z, high, 0, 1, z] = -s
            by_y[:, 1, y, z, high, 0, 1, z] = c
            by_y[:, 0, y, z, high, 1, 0, z] = s
            by_y[:, 1, y, z, high, 1, 0, z] = -c
            by_y[:, 0, y, z, high, 1, 1, z] = c
            by_y[:, 1, y, z, high, 1, 1, z] = s
    return (
        rounded(by_z.reshape(256, 256)),
        rounded(by_x.reshape(512, 1024)),
        rounded(by_h.reshape(512, 512)),
        rounded(by_y.reshape(16, 256, 256)),
    )


def dot(a, b):
    return jnp.dot(a, b, preferred_element_type=F32)


def root(count):
    angle = (count - 64.0 * jnp.floor(count / 64.0)) * (TWO_PI / 64.0)
    return jnp.cos(angle), jnp.sin(angle)


def halves(x):
    high = x.astype(BF16).astype(F32)
    return high, x - high


def factors(facts):
    defocus, sx, sy, sz = (facts[:, i : i + 1] for i in range(1, 5))
    cell = lax.broadcasted_iota(jnp.int32, (ROWS, CELLS), 1)
    kx = (cell // BAND - BAND // 2).astype(F32)
    ky = (cell % BAND - BAND // 2).astype(F32)
    focus = defocus * (kx * kx + ky * ky) / BAND + 0.3
    cos_a, sin_a = root(kx * sx + ky * sy)
    cos_f, sin_f = jnp.cos(focus), jnp.sin(focus)
    rows = [halves(x) for x in (sin_f * cos_a, sin_f * sin_a, cos_f * cos_a, cos_f * sin_a)]
    lane = lax.broadcasted_iota(jnp.int32, (ROWS, LANES), 1)
    kz = (lane % BAND - BAND // 2).astype(F32)
    cos_b, sin_b = root(kz * sz)
    first = lane < LANES // 2
    one = jnp.where(first, cos_b, sin_b)
    two = jnp.where(first, -sin_b, cos_b)
    focus = defocus * (kz * kz) / BAND
    cos_f, sin_f = jnp.cos(focus), jnp.sin(focus)
    lanes = [halves(x) for x in (cos_f * one, cos_f * two, sin_f * one, sin_f * two)]
    blank = jnp.zeros((32, CELLS), F32)
    left = jnp.concatenate(
        [r[0] for r in rows] + [r[0] for r in rows] + [r[1] for r in rows] + [blank], axis=0
    )
    right = jnp.concatenate(
        [x[0] for x in lanes] + [x[1] for x in lanes] + [x[0] for x in lanes] + [blank[:, :LANES]], axis=0
    )
    owner = lax.broadcasted_iota(jnp.int32, (LANES, LANES), 0) % ROWS
    right = [jnp.where(owner == p, right, 0.0) for p in range(ROWS)]
    return left.T.astype(BF16), jnp.concatenate(right, axis=1).astype(BF16)


def collect(labels, defocus, shifts):
    row = lax.broadcasted_iota(jnp.int32, (ROWS, LANES), 0)
    lane = lax.broadcasted_iota(jnp.int32, (ROWS, LANES), 1)
    facts = jnp.zeros((ROWS, LANES), F32)
    for p in range(ROWS):
        values = [labels[p].astype(F32), defocus[p]] + [shifts[i, p].astype(F32) for i in range(3)]
        for i, value in enumerate(values):
            facts = jnp.where((row == p) & (lane == i), value, facts)
    return facts


def whole(owners, turn_ref, label_ref, defocus_ref, shift_ref, vol_hbm, rot_hbm, refs_hbm,
          z_hbm, x_hbm, h_hbm, y_hbm, new_ref, score_ref,
          vol_ref, rot_ref, refs_ref, z_ref, x_ref, h_ref, y_ref,
          by_z, by_x, by_h, spec, left_ref, right_ref, wide, energy_ref,
          send, held, facts_ref, facts, chosen, below, parts, answer, load_sems, fact_sems, data_sems, answer_sems):
    me = lax.axis_index("dev")
    class_count, columns = refs_ref.shape
    pairs = columns // LANES
    particles = owners * ROWS

    def load(i):
        if i < CHUNKS:
            at = pl.ds(i * (4096 // CHUNKS), 4096 // CHUNKS)
            src, dst = vol_hbm.at[:, at], vol_ref.at[:, at]
        else:
            src, dst = (
                (z_hbm, z_ref), (x_hbm, x_ref), (h_hbm, h_ref), (y_hbm, y_ref), (rot_hbm, rot_ref), (refs_hbm, refs_ref)
            )[i - CHUNKS]
        return pltpu.make_async_copy(src, dst, load_sems.at[i])

    for i in (CHUNKS, *range(CHUNKS), *range(CHUNKS + 1, CHUNKS + 6)):
        load(i).start()

    def remote(src, dst, sems, to, k):
        return pltpu.make_async_remote_copy(
            src_ref=src, dst_ref=dst, send_sem=sems.at[0, k], recv_sem=sems.at[1, k],
            device_id={"dev": to}, device_id_type=pl.DeviceIdType.MESH,
        )

    def fact_copy(k):
        return remote(facts_ref, facts.at[me], fact_sems, lax.rem(me + k, owners), k)

    def data_copy(g, k):
        to = lax.rem(me + k, owners)
        at = pl.ds(g * GROUP, GROUP)
        return remote(send.at[to, at], held.at[me, at], data_sems.at[g], to, k)

    def answer_copy(k):
        to = lax.rem(me + k, owners)
        return remote(parts.at[to], answer.at[me], answer_sems, to, k)

    barrier = pltpu.get_barrier_semaphore()

    @pl.loop(1, owners)
    def _(k):
        pl.semaphore_signal(
            barrier, inc=1, device_id={"dev": lax.rem(me + k, owners)}, device_id_type=pl.DeviceIdType.MESH
        )

    own_facts = collect(label_ref, defocus_ref, shift_ref)
    facts_ref[...] = own_facts
    left, right = factors(own_facts)
    left_ref[...] = left
    right_ref[...] = right

    load(CHUNKS).wait()
    for chunk in range(CHUNKS):
        load(chunk).wait()

        @pl.loop(chunk * (16 // CHUNKS), (chunk + 1) * (16 // CHUNKS), unroll=2)
        def _(h):
            got = dot(vol_ref[:, pl.ds(pl.multiple_of(h * 256, 256), 256)], z_ref[...]).astype(BF16)
            at = pl.ds(pl.multiple_of(h * 128, 128), 128)
            by_z[0:512, at] = got[:, :128]
            by_z[512:1024, at] = got[:, 128:]

    load(CHUNKS + 1).wait()

    @pl.loop(0, 8)
    def _(h2):
        got = dot(x_ref[...], by_z[:, pl.ds(pl.multiple_of(h2 * 256, 256), 256)]).astype(BF16)
        for i in range(2):
            to = pl.ds(pl.multiple_of(h2 * 64 + i * 32, 32), 32)
            for g in range(16):
                by_x[to, g * 128 : (g + 1) * 128] = got[g * 32 : (g + 1) * 32, i * 128 : (i + 1) * 128]

    pl.semaphore_wait(barrier, owners - 1)

    @pl.loop(1, owners)
    def _(k):
        fact_copy(k).start()

    facts[me] = facts_ref[...]
    load(CHUNKS + 2).wait()

    @pl.loop(0, 8)
    def _(g2):
        got = dot(h_ref[...], by_x[:, pl.ds(pl.multiple_of(g2 * 256, 256), 256)]).astype(BF16)
        got = got.reshape(16, 2, 16, 256)
        for i in range(2):
            to = pl.ds(pl.multiple_of(g2 * 32 + i * 16, 16), 16)
            for c in range(2):
                by_h[:, to, c * 128 : (c + 1) * 128] = got[:, c, :, i * 128 : (i + 1) * 128]

    load(CHUNKS + 3).wait()

    @pl.loop(0, 16, unroll=2)
    def _(q):
        got = dot(by_h[q], y_ref[q])
        for high in range(2):
            spec[pl.ds(high * 16 + q, 256, stride=32), :] = got[:, high * 128 : (high + 1) * 128]

    load(CHUNKS + 4).wait()
    first = lax.broadcasted_iota(jnp.int32, (CELLS // 2, LANES), 1) < LANES // 2

    @pl.loop(0, ROWS // GROUP)
    def _(g):
        @pl.loop(0, GROUP)
        def _(within):
            p = g * GROUP + within
            own = spec[pl.ds(pl.multiple_of(p * CELLS, CELLS), CELLS), :].astype(BF16)
            turned = dot(rot_ref[turn_ref[p]], own)
            factor = dot(left_ref[...], right_ref[:, pl.ds(pl.multiple_of(p * 128, 128), 128)])
            both = turned * factor
            wide[0:CELLS, :] = both + pltpu.roll(both, LANES // 2, 1)
            even = wide[pl.ds(0, CELLS // 2, stride=2), :]
            odd = wide[pl.ds(1, CELLS // 2, stride=2), :]
            packed = jnp.where(first, even, odd).astype(BF16)
            send[:, p] = packed.reshape(owners, pairs, LANES)
            long = packed.astype(F32)
            energy_ref[pl.ds(p, 1), :] = jnp.sum(long * long, axis=0, keepdims=True)

        @pl.loop(1, owners)
        def _(k):
            data_copy(g, k).start()

    held[me] = send[me]

    @pl.loop(1, owners)
    def _(k):
        fact_copy(k).wait()

    load(CHUNKS + 5).wait()
    known = facts[...].reshape(particles, LANES)
    lane = lax.broadcasted_iota(jnp.int32, (particles, LANES), 1)
    member = jnp.where(known[:, 0:1] == lane.astype(F32), 1.0, 0.0)
    across = member.T[:class_count]
    defocus = known[:, 1:2]
    one = lax.broadcasted_iota(jnp.int32, (1, LANES), 1)
    kz = one % BAND - BAND // 2

    @pl.loop(0, pairs, unroll=2)
    def _(r):
        cell = (me * pairs + r) * 2 + one // (2 * BAND)
        kx = cell // BAND - BAND // 2
        ky = cell % BAND - BAND // 2
        radius = (kx * kx + ky * ky + kz * kz).astype(F32)
        weight = jnp.sin(defocus * radius / BAND + 0.3)
        total = jnp.dot(across, weight * weight, preferred_element_type=F32, precision=lax.Precision.HIGHEST)
        below[r] = 1.0 / (total + 1.0)
        at = pl.ds(pl.multiple_of(r * LANES, LANES), LANES)
        chosen[r] = dot(member[:, :class_count].astype(BF16), refs_ref[:, at])

    @pl.loop(0, ROWS // GROUP)
    def _(g):
        @pl.loop(1, owners)
        def _(k):
            data_copy(g, k).wait()

    wide[0 : particles * pairs, :] = held[...].astype(F32).reshape(particles * pairs, LANES)
    parts[...] = jnp.zeros_like(parts)

    @pl.loop(0, pairs, unroll=4)
    def _(r):
        rows = wide[pl.ds(r, particles, stride=pairs), :]
        total = dot(across.astype(BF16), rows.astype(BF16))
        new_ref[:, pl.ds(pl.multiple_of(r * LANES, LANES), LANES)] = total * below[r]
        parts[...] += (rows * chosen[r]).reshape(owners, ROWS, LANES)

    @pl.loop(1, owners)
    def _(k):
        answer_copy(k).start()

    answer[me] = parts[me]

    @pl.loop(1, owners)
    def _(k):
        answer_copy(k).wait()

    agreement = jnp.sum(jnp.sum(answer[...], axis=0), axis=1, keepdims=True)
    energy = jnp.sum(energy_ref[...], axis=1, keepdims=True)
    score_ref[...] = jnp.broadcast_to(agreement / jnp.sqrt(energy + 1e-06), (ROWS, LANES))


def on_device(owners, volumes, rotations, turn_ids, shifts, defocus, labels, references):
    class_count, columns = references.shape
    pairs = columns // LANES
    particles = owners * ROWS
    rows = volumes.reshape(ROWS, BOX, BOX * BOX).transpose(1, 0, 2).reshape(BOX * ROWS, BOX * BOX)
    constants = [jnp.asarray(t) for t in tables()]
    new_refs, scores = pl.pallas_call(
        lambda *refs: whole(owners, *refs),
        out_shape=(
            jax.ShapeDtypeStruct((class_count, columns), F32),
            jax.ShapeDtypeStruct((ROWS, LANES), F32),
        ),
        in_specs=[SMEM] * 4 + [HBM] * 7,
        out_specs=(VMEM, VMEM),
        scratch_shapes=[
            pltpu.VMEM(x.shape, BF16) for x in (rows, rotations, references, *constants)
        ] + [
            pltpu.VMEM((1024, 2048), BF16),
            pltpu.VMEM((512, 2048), BF16),
            pltpu.VMEM((16, 256, 256), BF16),
            pltpu.VMEM((ROWS * CELLS, LANES), F32),
            pltpu.VMEM((CELLS, LANES), BF16),
            pltpu.VMEM((LANES, ROWS * LANES), BF16),
            pltpu.VMEM((max(CELLS, particles * pairs), LANES), F32),
            pltpu.VMEM((ROWS, LANES), F32),
            pltpu.VMEM((owners, ROWS, pairs, LANES), BF16),
            pltpu.VMEM((owners, ROWS, pairs, LANES), BF16),
            pltpu.VMEM((ROWS, LANES), F32),
            pltpu.VMEM((owners, ROWS, LANES), F32),
            pltpu.VMEM((pairs, particles, LANES), F32),
            pltpu.VMEM((pairs, class_count, LANES), F32),
            pltpu.VMEM((owners, ROWS, LANES), F32),
            pltpu.VMEM((owners, ROWS, LANES), F32),
            pltpu.SemaphoreType.DMA((CHUNKS + 6,)),
            pltpu.SemaphoreType.DMA((2, owners)),
            pltpu.SemaphoreType.DMA((ROWS // GROUP, 2, owners)),
            pltpu.SemaphoreType.DMA((2, owners)),
        ],
        compiler_params=pltpu.CompilerParams(
            collective_id=0, has_side_effects=True, vmem_limit_bytes=52 * 1024 * 1024
        ),
    )(turn_ids, labels, defocus, shifts.T, rows, rotations, references, *constants)
    return new_refs, scores[:, 0]


def solution(mesh):
    owners = mesh.shape["dev"]
    return jax.shard_map(
        lambda *args: on_device(owners, *args),
        mesh=mesh,
        in_specs=(
            P(("groups", "dev"), None),
            P(),
            P(("groups", "dev")),
            P(("groups", "dev"), None),
            P(("groups", "dev")),
            P(("groups", "dev")),
            P("groups", "dev"),
        ),
        out_specs=(P("groups", "dev"), P(("groups", "dev"))),
        check_vma=False,
    )
```

```python
import math

import jax
import jax.numpy as jnp
import ml_dtypes
import numpy as np
from jax import lax
from jax.experimental import pallas as pl
from jax.experimental.pallas import tpu as pltpu
from jax.sharding import PartitionSpec as P

BOX = 64
BAND = 32
ROWS = 8
CELLS = BAND * BAND
LANES = 128
CHUNKS = 4
GROUP = 2
STEPS = 4
STEP = ROWS // STEPS
TWO_PI = 2.0 * math.pi
VMEM = pl.BlockSpec(memory_space=pltpu.VMEM)
HBM = pl.BlockSpec(memory_space=pltpu.HBM)
SMEM = pl.BlockSpec(memory_space=pltpu.SMEM)
F32 = jnp.float32
BF16 = jnp.bfloat16


def rounded(table):
    table = np.asarray(table, np.float32).astype(ml_dtypes.bfloat16)
    return table.reshape(*table.shape[:-2], -1, 8, table.shape[-1])


def tables():
    n = np.arange(BOX)
    k = np.arange(BAND) - BAND // 2
    angle = TWO_PI * ((n[:, None] * k[None, :]) % BOX) / BOX
    cosine, sine = np.cos(angle) / 8.0, np.sin(angle) / 8.0
    by_z = np.zeros((4, 64, 2, 4, 32))
    for y in range(4):
        by_z[y, :, 0, y] = cosine
        by_z[y, :, 1, y] = -sine
    mixing = np.array([[cosine, sine], [-sine, cosine]])
    by_x = np.zeros((8, 2, 2, 16, 2, 64, 8))
    for p in range(8):
        by_x[p, :, :, :, :, :, p] = mixing.reshape(2, 2, 64, 2, 16).transpose(3, 0, 4, 1, 2)
    q = np.arange(16)
    turn = TWO_PI * ((q[:, None] * q[None, :]) % 16) / 16
    c, s = np.cos(turn) / 4.0, np.sin(turn) / 4.0
    by_h = np.zeros((16, 2, 16, 16, 2, 16))
    for low in range(16):
        by_h[:, 0, low, :, 0, low] = c
        by_h[:, 0, low, :, 1, low] = s
        by_h[:, 1, low, :, 0, low] = -s
        by_h[:, 1, low, :, 1, low] = c
    by_y = np.zeros((16, 2, 4, 32, 2, 2, 2, 32))
    for high in range(2):
        for y in range(4):
            part = TWO_PI * (((high * 16 + q - 16) * y) % 64) / 64
            c, s = (np.cos(part) / 2.0)[:, None], (np.sin(part) / 2.0)[:, None]
            z = np.arange(32)
            by_y[:, 0, y, z, high, 0, 0, z] = c
            by_y[:, 1, y, z, high, 0, 0, z] = s
            by_y[:, 0, y, z, high, 0, 1, z] = -s
            by_y[:, 1, y, z, high, 0, 1, z] = c
            by_y[:, 0, y, z, high, 1, 0, z] = s
            by_y[:, 1, y, z, high, 1, 0, z] = -c
            by_y[:, 0, y, z, high, 1, 1, z] = c
            by_y[:, 1, y, z, high, 1, 1, z] = s
    return (
        rounded(by_z.reshape(256, 256)),
        rounded(by_x.reshape(512, 1024)),
        rounded(by_h.reshape(512, 512)),
        rounded(by_y.reshape(16, 256, 256)),
    )


def dot(a, b):
    return jnp.dot(a, b, preferred_element_type=F32)


def root(count):
    angle = (count - 64.0 * jnp.floor(count / 64.0)) * (TWO_PI / 64.0)
    return jnp.cos(angle), jnp.sin(angle)


def halves(x):
    high = x.astype(BF16).astype(F32)
    return high, x - high


def factors(facts):
    defocus, sx, sy, sz = (facts[:, i : i + 1] for i in range(1, 5))
    cell = lax.broadcasted_iota(jnp.int32, (ROWS, CELLS), 1)
    kx = (cell // BAND - BAND // 2).astype(F32)
    ky = (cell % BAND - BAND // 2).astype(F32)
    focus = defocus * (kx * kx + ky * ky) / BAND + 0.3
    cos_a, sin_a = root(kx * sx + ky * sy)
    cos_f, sin_f = jnp.cos(focus), jnp.sin(focus)
    rows = [halves(x) for x in (sin_f * cos_a, sin_f * sin_a, cos_f * cos_a, cos_f * sin_a)]
    lane = lax.broadcasted_iota(jnp.int32, (ROWS, LANES), 1)
    kz = (lane % BAND - BAND // 2).astype(F32)
    cos_b, sin_b = root(kz * sz)
    first = lane < LANES // 2
    one = jnp.where(first, cos_b, sin_b)
    two = jnp.where(first, -sin_b, cos_b)
    focus = defocus * (kz * kz) / BAND
    cos_f, sin_f = jnp.cos(focus), jnp.sin(focus)
    lanes = [halves(x) for x in (cos_f * one, cos_f * two, sin_f * one, sin_f * two)]
    blank = jnp.zeros((32, CELLS), F32)
    left = jnp.concatenate(
        [r[0] for r in rows] + [r[0] for r in rows] + [r[1] for r in rows] + [blank], axis=0
    )
    right = jnp.concatenate(
        [x[0] for x in lanes] + [x[1] for x in lanes] + [x[0] for x in lanes] + [blank[:, :LANES]], axis=0
    )
    owner = lax.broadcasted_iota(jnp.int32, (LANES, LANES), 0) % ROWS
    right = [jnp.where(owner == p, right, 0.0) for p in range(ROWS)]
    return left.T.astype(BF16), jnp.concatenate(right, axis=1).astype(BF16)


def collect(labels, defocus, shifts):
    row = lax.broadcasted_iota(jnp.int32, (ROWS, LANES), 0)
    lane = lax.broadcasted_iota(jnp.int32, (ROWS, LANES), 1)
    facts = jnp.zeros((ROWS, LANES), F32)
    for p in range(ROWS):
        values = [labels[p].astype(F32), defocus[p]] + [shifts[i, p].astype(F32) for i in range(3)]
        for i, value in enumerate(values):
            facts = jnp.where((row == p) & (lane == i), value, facts)
    return facts


def whole(owners, turn_ref, label_ref, defocus_ref, shift_ref, vol_hbm, rot_hbm, refs_hbm,
          z_hbm, x_hbm, h_hbm, y_hbm, new_ref, score_ref,
          vol_ref, rot_ref, refs_ref, z_ref, x_ref, h_ref, y_ref,
          by_z, by_x, by_h, spec, left_ref, right_ref, wide, energy_ref,
          send, held, facts_ref, facts, chosen, below, parts, answer, load_sems, fact_sems, data_sems, answer_sems):
    me = lax.axis_index("dev")
    class_count, columns = refs_ref.shape
    pairs = columns // LANES
    particles = owners * ROWS

    def load(i):
        if i < CHUNKS:
            at = pl.ds(i * (4096 // CHUNKS), 4096 // CHUNKS)
            src, dst = vol_hbm.at[:, at], vol_ref.at[:, at]
        else:
            src, dst = (
                (z_hbm, z_ref), (x_hbm, x_ref), (h_hbm, h_ref), (y_hbm, y_ref), (rot_hbm, rot_ref), (refs_hbm, refs_ref)
            )[i - CHUNKS]
        return pltpu.make_async_copy(src, dst, load_sems.at[i])

    for i in (CHUNKS, *range(CHUNKS), *range(CHUNKS + 1, CHUNKS + 6)):
        load(i).start()

    def remote(src, dst, sems, to, k):
        return pltpu.make_async_remote_copy(
            src_ref=src, dst_ref=dst, send_sem=sems.at[0, k], recv_sem=sems.at[1, k],
            device_id={"dev": to}, device_id_type=pl.DeviceIdType.MESH,
        )

    def fact_copy(k):
        return remote(facts_ref, facts.at[me], fact_sems, lax.rem(me + k, owners), k)

    def data_copy(g, k):
        to = lax.rem(me + k, owners)
        at = pl.ds(g * GROUP, GROUP)
        return remote(send.at[to, at], held.at[me, at], data_sems.at[g], to, k)

    def answer_copy(k):
        to = lax.rem(me + k, owners)
        return remote(parts.at[to], answer.at[me], answer_sems, to, k)

    barrier = pltpu.get_barrier_semaphore()

    @pl.loop(1, owners)
    def _(k):
        pl.semaphore_signal(
            barrier, inc=1, device_id={"dev": lax.rem(me + k, owners)}, device_id_type=pl.DeviceIdType.MESH
        )

    own_facts = collect(label_ref, defocus_ref, shift_ref)
    facts_ref[...] = own_facts
    left, right = factors(own_facts)
    left_ref[...] = left
    right_ref[...] = right

    load(CHUNKS).wait()
    for chunk in range(CHUNKS):
        load(chunk).wait()

        @pl.loop(chunk * (16 // CHUNKS), (chunk + 1) * (16 // CHUNKS), unroll=2)
        def _(h):
            got = dot(vol_ref[:, pl.ds(pl.multiple_of(h * 256, 256), 256)], z_ref[...].reshape(256, 256)).astype(BF16)
            at = pl.ds(pl.multiple_of(h * 128, 128), 128)
            by_z[0:512, at] = got[:, :128]
            by_z[512:1024, at] = got[:, 128:]

    load(CHUNKS + 1).wait()

    @pl.loop(0, 8, unroll=2)
    def _(h2):
        got = dot(x_ref[...].reshape(512, 1024), by_z[:, pl.ds(pl.multiple_of(h2 * 256, 256), 256)]).astype(BF16)
        for i in range(2):
            to = pl.ds(pl.multiple_of(h2 * 64 + i * 32, 32), 32)
            for g in range(16):
                by_x[to, g * 128 : (g + 1) * 128] = got[g * 32 : (g + 1) * 32, i * 128 : (i + 1) * 128]

    pl.semaphore_wait(barrier, owners - 1)

    @pl.loop(1, owners)
    def _(k):
        fact_copy(k).start()

    facts[me] = facts_ref[...]
    first = lax.broadcasted_iota(jnp.int32, (CELLS // 2, LANES), 1) < LANES // 2
    for i in (2, 3, 4):
        load(CHUNKS + i).wait()

    @pl.loop(0, STEPS)
    def _(step):
        @pl.loop(0, STEP, unroll=min(STEP, 2))
        def _(within):
            p = step * STEP + within
            got = dot(h_ref[...].reshape(512, 512), by_x[:, pl.ds(pl.multiple_of(p * 256, 256), 256)]).astype(BF16)
            got = got.reshape(16, 2, 16, 256)
            for i in range(2):
                to = pl.ds(pl.multiple_of(p * 32 + i * 16, 16), 16)
                for c in range(2):
                    by_h[:, to, c * 128 : (c + 1) * 128] = got[:, c, :, i * 128 : (i + 1) * 128]

        @pl.loop(0, 16, unroll=4)
        def _(q):
            own = by_h[q, pl.ds(pl.multiple_of(step * STEP * 32, STEP * 32), STEP * 32), :]
            got = dot(own, y_ref[q].reshape(256, 256))
            for high in range(2):
                to = pl.ds(step * STEP * CELLS + high * 16 + q, STEP * 32, stride=32)
                spec[to, :] = got[:, high * 128 : (high + 1) * 128]

        @pl.loop(step * (STEP // GROUP), (step + 1) * (STEP // GROUP))
        def _(g):
            @pl.loop(0, GROUP)
            def _(within):
                p = g * GROUP + within
                own = spec[pl.ds(pl.multiple_of(p * CELLS, CELLS), CELLS), :].astype(BF16)
                turned = dot(rot_ref[turn_ref[p]], own)
                factor = dot(left_ref[...], right_ref[:, pl.ds(pl.multiple_of(p * 128, 128), 128)])
                both = turned * factor
                wide[0:CELLS, :] = both + pltpu.roll(both, LANES // 2, 1)
                even = wide[pl.ds(0, CELLS // 2, stride=2), :]
                odd = wide[pl.ds(1, CELLS // 2, stride=2), :]
                packed = jnp.where(first, even, odd).astype(BF16)
                send[:, p] = packed.reshape(owners, pairs, LANES)
                long = packed.astype(F32)
                energy_ref[pl.ds(p, 1), :] = jnp.sum(long * long, axis=0, keepdims=True)

            @pl.loop(1, owners)
            def _(k):
                data_copy(g, k).start()

    held[me] = send[me]

    @pl.loop(1, owners)
    def _(k):
        fact_copy(k).wait()

    load(CHUNKS + 5).wait()
    known = facts[...].reshape(particles, LANES)
    lane = lax.broadcasted_iota(jnp.int32, (particles, LANES), 1)
    member = jnp.where(known[:, 0:1] == lane.astype(F32), 1.0, 0.0)
    across = member.T[:class_count]
    defocus = known[:, 1:2]
    one = lax.broadcasted_iota(jnp.int32, (1, LANES), 1)
    kz = one % BAND - BAND // 2

    @pl.loop(0, pairs, unroll=2)
    def _(r):
        cell = (me * pairs + r) * 2 + one // (2 * BAND)
        kx = cell // BAND - BAND // 2
        ky = cell % BAND - BAND // 2
        radius = (kx * kx + ky * ky + kz * kz).astype(F32)
        weight = jnp.sin(defocus * radius / BAND + 0.3)
        total = jnp.dot(across, weight * weight, preferred_element_type=F32, precision=lax.Precision.HIGHEST)
        below[r] = 1.0 / (total + 1.0)
        at = pl.ds(pl.multiple_of(r * LANES, LANES), LANES)
        chosen[r] = dot(member[:, :class_count].astype(BF16), refs_ref[:, at])

    @pl.loop(0, ROWS // GROUP)
    def _(g):
        @pl.loop(1, owners)
        def _(k):
            data_copy(g, k).wait()

    wide[0 : particles * pairs, :] = held[...].astype(F32).reshape(particles * pairs, LANES)
    parts[...] = jnp.zeros_like(parts)

    @pl.loop(0, pairs, unroll=4)
    def _(r):
        rows = wide[pl.ds(r, particles, stride=pairs), :]
        parts[...] += (rows * chosen[r]).reshape(owners, ROWS, LANES)

    @pl.loop(1, owners)
    def _(k):
        answer_copy(k).start()

    answer[me] = parts[me]

    @pl.loop(0, pairs, unroll=4)
    def _(r):
        rows = wide[pl.ds(r, particles, stride=pairs), :]
        total = dot(across.astype(BF16), rows.astype(BF16))
        new_ref[:, pl.ds(pl.multiple_of(r * LANES, LANES), LANES)] = total * below[r]

    @pl.loop(1, owners)
    def _(k):
        answer_copy(k).wait()

    agreement = jnp.sum(jnp.sum(answer[...], axis=0), axis=1, keepdims=True)
    energy = jnp.sum(energy_ref[...], axis=1, keepdims=True)
    score_ref[...] = jnp.broadcast_to(agreement / jnp.sqrt(energy + 1e-06), (ROWS, LANES))


def on_device(owners, volumes, rotations, turn_ids, shifts, defocus, labels, references):
    class_count, columns = references.shape
    pairs = columns // LANES
    particles = owners * ROWS
    rows = volumes.reshape(ROWS, BOX, BOX * BOX).transpose(1, 0, 2).reshape(BOX * ROWS, BOX * BOX)
    constants = [jnp.asarray(t) for t in tables()]
    new_refs, scores = pl.pallas_call(
        lambda *refs: whole(owners, *refs),
        out_shape=(
            jax.ShapeDtypeStruct((class_count, columns), F32),
            jax.ShapeDtypeStruct((ROWS, LANES), F32),
        ),
        in_specs=[SMEM] * 4 + [HBM] * 7,
        out_specs=(VMEM, VMEM),
        scratch_shapes=[
            pltpu.VMEM(x.shape, BF16) for x in (rows, rotations, references, *constants)
        ] + [
            pltpu.VMEM((1024, 2048), BF16),
            pltpu.VMEM((512, 2048), BF16),
            pltpu.VMEM((16, 256, 256), BF16),
            pltpu.VMEM((ROWS * CELLS, LANES), F32),
            pltpu.VMEM((CELLS, LANES), BF16),
            pltpu.VMEM((LANES, ROWS * LANES), BF16),
            pltpu.VMEM((max(CELLS, particles * pairs), LANES), F32),
            pltpu.VMEM((ROWS, LANES), F32),
            pltpu.VMEM((owners, ROWS, pairs, LANES), BF16),
            pltpu.VMEM((owners, ROWS, pairs, LANES), BF16),
            pltpu.VMEM((ROWS, LANES), F32),
            pltpu.VMEM((owners, ROWS, LANES), F32),
            pltpu.VMEM((pairs, particles, LANES), F32),
            pltpu.VMEM((pairs, class_count, LANES), F32),
            pltpu.VMEM((owners, ROWS, LANES), F32),
            pltpu.VMEM((owners, ROWS, LANES), F32),
            pltpu.SemaphoreType.DMA((CHUNKS + 6,)),
            pltpu.SemaphoreType.DMA((2, owners)),
            pltpu.SemaphoreType.DMA((ROWS // GROUP, 2, owners)),
            pltpu.SemaphoreType.DMA((2, owners)),
        ],
        compiler_params=pltpu.CompilerParams(
            collective_id=0, has_side_effects=True, vmem_limit_bytes=64 * 1024 * 1024
        ),
    )(turn_ids, labels, defocus, shifts.T, rows, rotations, references, *constants)
    return new_refs, scores[:, 0]


def solution(mesh):
    owners = mesh.shape["dev"]
    return jax.shard_map(
        lambda *args: on_device(owners, *args),
        mesh=mesh,
        in_specs=(
            P(("groups", "dev"), None),
            P(),
            P(("groups", "dev")),
            P(("groups", "dev"), None),
            P(("groups", "dev")),
            P(("groups", "dev")),
            P("groups", "dev"),
        ),
        out_specs=(P("groups", "dev"), P(("groups", "dev"))),
        check_vma=False,
    )
```

```python
import math

import jax
import jax.numpy as jnp
import ml_dtypes
import numpy as np
from jax import lax
from jax.experimental import pallas as pl
from jax.experimental.pallas import tpu as pltpu
from jax.sharding import PartitionSpec as P

BOX = 64
BAND = 32
ROWS = 8
CELLS = BAND * BAND
LANES = 128
CHUNKS = 8
GROUP = 2
STEPS = 4
STEP = ROWS // STEPS
TWO_PI = 2.0 * math.pi
VMEM = pl.BlockSpec(memory_space=pltpu.VMEM)
HBM = pl.BlockSpec(memory_space=pltpu.HBM)
SMEM = pl.BlockSpec(memory_space=pltpu.SMEM)
F32 = jnp.float32
BF16 = jnp.bfloat16


def rounded(table):
    table = np.asarray(table, np.float32).astype(ml_dtypes.bfloat16)
    return table.reshape(*table.shape[:-2], -1, 8, table.shape[-1])


def tables():
    n = np.arange(BOX)
    k = np.arange(BAND) - BAND // 2
    angle = TWO_PI * ((n[:, None] * k[None, :]) % BOX) / BOX
    cosine, sine = np.cos(angle) / 8.0, np.sin(angle) / 8.0
    by_z = np.zeros((4, 64, 2, 4, 32))
    for y in range(4):
        by_z[y, :, 0, y] = cosine
        by_z[y, :, 1, y] = -sine
    mixing = np.array([[cosine, sine], [-sine, cosine]])
    by_x = np.zeros((8, 2, 2, 16, 2, 64, 8))
    for p in range(8):
        by_x[p, :, :, :, :, :, p] = mixing.reshape(2, 2, 64, 2, 16).transpose(3, 0, 4, 1, 2)
    q = np.arange(16)
    turn = TWO_PI * ((q[:, None] * q[None, :]) % 16) / 16
    c, s = np.cos(turn) / 4.0, np.sin(turn) / 4.0
    by_h = np.zeros((16, 2, 16, 16, 2, 16))
    for low in range(16):
        by_h[:, 0, low, :, 0, low] = c
        by_h[:, 0, low, :, 1, low] = s
        by_h[:, 1, low, :, 0, low] = -s
        by_h[:, 1, low, :, 1, low] = c
    by_y = np.zeros((16, 2, 4, 32, 2, 2, 2, 32))
    for high in range(2):
        for y in range(4):
            part = TWO_PI * (((high * 16 + q - 16) * y) % 64) / 64
            c, s = (np.cos(part) / 2.0)[:, None], (np.sin(part) / 2.0)[:, None]
            z = np.arange(32)
            by_y[:, 0, y, z, high, 0, 0, z] = c
            by_y[:, 1, y, z, high, 0, 0, z] = s
            by_y[:, 0, y, z, high, 0, 1, z] = -s
            by_y[:, 1, y, z, high, 0, 1, z] = c
            by_y[:, 0, y, z, high, 1, 0, z] = s
            by_y[:, 1, y, z, high, 1, 0, z] = -c
            by_y[:, 0, y, z, high, 1, 1, z] = c
            by_y[:, 1, y, z, high, 1, 1, z] = s
    return (
        rounded(by_z.reshape(256, 256)),
        rounded(by_x.reshape(512, 1024)),
        rounded(by_h.reshape(512, 512)),
        rounded(by_y.reshape(16, 256, 256)),
    )


def dot(a, b):
    return jnp.dot(a, b, preferred_element_type=F32)


def root(count):
    angle = (count - 64.0 * jnp.floor(count / 64.0)) * (TWO_PI / 64.0)
    return jnp.cos(angle), jnp.sin(angle)


def halves(x):
    high = x.astype(BF16).astype(F32)
    return high, x - high


def factors(facts):
    defocus, sx, sy, sz = (facts[:, i : i + 1] for i in range(1, 5))
    cell = lax.broadcasted_iota(jnp.int32, (ROWS, CELLS), 1)
    kx = (cell // BAND - BAND // 2).astype(F32)
    ky = (cell % BAND - BAND // 2).astype(F32)
    focus = defocus * (kx * kx + ky * ky) / BAND + 0.3
    cos_a, sin_a = root(kx * sx + ky * sy)
    cos_f, sin_f = jnp.cos(focus), jnp.sin(focus)
    rows = [halves(x) for x in (sin_f * cos_a, sin_f * sin_a, cos_f * cos_a, cos_f * sin_a)]
    lane = lax.broadcasted_iota(jnp.int32, (ROWS, LANES), 1)
    kz = (lane % BAND - BAND // 2).astype(F32)
    cos_b, sin_b = root(kz * sz)
    first = lane < LANES // 2
    one = jnp.where(first, cos_b, sin_b)
    two = jnp.where(first, -sin_b, cos_b)
    focus = defocus * (kz * kz) / BAND
    cos_f, sin_f = jnp.cos(focus), jnp.sin(focus)
    lanes = [halves(x) for x in (cos_f * one, cos_f * two, sin_f * one, sin_f * two)]
    blank = jnp.zeros((32, CELLS), F32)
    left = jnp.concatenate(
        [r[0] for r in rows] + [r[0] for r in rows] + [r[1] for r in rows] + [blank], axis=0
    )
    right = jnp.concatenate(
        [x[0] for x in lanes] + [x[1] for x in lanes] + [x[0] for x in lanes] + [blank[:, :LANES]], axis=0
    )
    owner = lax.broadcasted_iota(jnp.int32, (LANES, LANES), 0) % ROWS
    right = [jnp.where(owner == p, right, 0.0) for p in range(ROWS)]
    return left.T.astype(BF16), jnp.concatenate(right, axis=1).astype(BF16)


def collect(labels, defocus, shifts):
    row = lax.broadcasted_iota(jnp.int32, (ROWS, LANES), 0)
    lane = lax.broadcasted_iota(jnp.int32, (ROWS, LANES), 1)
    facts = jnp.zeros((ROWS, LANES), F32)
    for p in range(ROWS):
        values = [labels[p].astype(F32), defocus[p]] + [shifts[i, p].astype(F32) for i in range(3)]
        for i, value in enumerate(values):
            facts = jnp.where((row == p) & (lane == i), value, facts)
    return facts


def whole(owners, turn_ref, label_ref, defocus_ref, shift_ref, vol_hbm, rot_hbm, refs_hbm,
          z_hbm, x_hbm, h_hbm, y_hbm, new_ref, score_ref,
          vol_ref, rot_ref, refs_ref, z_ref, x_ref, h_ref, y_ref,
          by_z, by_x, by_h, spec, left_ref, right_ref, wide, energy_ref,
          send, held, facts_ref, facts, chosen, below, parts, answer, load_sems, fact_sems, data_sems, answer_sems):
    me = lax.axis_index("dev")
    class_count, columns = refs_ref.shape
    pairs = columns // LANES
    particles = owners * ROWS

    def load(i):
        if i < CHUNKS:
            at = pl.ds(i * (4096 // CHUNKS), 4096 // CHUNKS)
            src, dst = vol_hbm.at[:, at], vol_ref.at[:, at]
        else:
            src, dst = (
                (z_hbm, z_ref), (x_hbm, x_ref), (h_hbm, h_ref), (y_hbm, y_ref), (rot_hbm, rot_ref), (refs_hbm, refs_ref)
            )[i - CHUNKS]
        return pltpu.make_async_copy(src, dst, load_sems.at[i])

    for i in (CHUNKS, *range(CHUNKS), *range(CHUNKS + 1, CHUNKS + 6)):
        load(i).start()

    def remote(src, dst, sems, to, k):
        return pltpu.make_async_remote_copy(
            src_ref=src, dst_ref=dst, send_sem=sems.at[0, k], recv_sem=sems.at[1, k],
            device_id={"dev": to}, device_id_type=pl.DeviceIdType.MESH,
        )

    def fact_copy(k):
        return remote(facts_ref, facts.at[me], fact_sems, lax.rem(me + k, owners), k)

    def data_copy(g, k):
        to = lax.rem(me + k, owners)
        at = pl.ds(g * GROUP, GROUP)
        return remote(send.at[to, at], held.at[me, at], data_sems.at[g], to, k)

    def answer_copy(k):
        to = lax.rem(me + k, owners)
        return remote(parts.at[to], answer.at[me], answer_sems, to, k)

    barrier = pltpu.get_barrier_semaphore()

    @pl.loop(1, owners)
    def _(k):
        pl.semaphore_signal(
            barrier, inc=1, device_id={"dev": lax.rem(me + k, owners)}, device_id_type=pl.DeviceIdType.MESH
        )

    own_facts = collect(label_ref, defocus_ref, shift_ref)
    facts_ref[...] = own_facts
    left, right = factors(own_facts)
    left_ref[...] = left
    right_ref[...] = right

    load(CHUNKS).wait()
    for chunk in range(CHUNKS):
        load(chunk).wait()

        @pl.loop(chunk * (16 // CHUNKS), (chunk + 1) * (16 // CHUNKS), unroll=2)
        def _(h):
            got = dot(vol_ref[:, pl.ds(pl.multiple_of(h * 256, 256), 256)], z_ref[...].reshape(256, 256)).astype(BF16)
            at = pl.ds(pl.multiple_of(h * 128, 128), 128)
            by_z[0:512, at] = got[:, :128]
            by_z[512:1024, at] = got[:, 128:]

    load(CHUNKS + 1).wait()

    @pl.loop(0, 8, unroll=4)
    def _(h2):
        got = dot(x_ref[...].reshape(512, 1024), by_z[:, pl.ds(pl.multiple_of(h2 * 256, 256), 256)]).astype(BF16)
        for i in range(2):
            to = pl.ds(pl.multiple_of(h2 * 64 + i * 32, 32), 32)
            for g in range(16):
                by_x[to, g * 128 : (g + 1) * 128] = got[g * 32 : (g + 1) * 32, i * 128 : (i + 1) * 128]

    pl.semaphore_wait(barrier, owners - 1)

    @pl.loop(1, owners)
    def _(k):
        fact_copy(k).start()

    facts[me] = facts_ref[...]
    first = lax.broadcasted_iota(jnp.int32, (CELLS // 2, LANES), 1) < LANES // 2
    for i in (2, 3, 4):
        load(CHUNKS + i).wait()

    @pl.loop(0, STEPS)
    def _(step):
        @pl.loop(0, STEP, unroll=min(STEP, 2))
        def _(within):
            p = step * STEP + within
            got = dot(h_ref[...].reshape(512, 512), by_x[:, pl.ds(pl.multiple_of(p * 256, 256), 256)]).astype(BF16)
            got = got.reshape(16, 2, 16, 256)
            for i in range(2):
                to = pl.ds(pl.multiple_of(p * 32 + i * 16, 16), 16)
                for c in range(2):
                    by_h[:, to, c * 128 : (c + 1) * 128] = got[:, c, :, i * 128 : (i + 1) * 128]

        @pl.loop(0, 16, unroll=8)
        def _(q):
            own = by_h[q, pl.ds(pl.multiple_of(step * STEP * 32, STEP * 32), STEP * 32), :]
            got = dot(own, y_ref[q].reshape(256, 256))
            for high in range(2):
                to = pl.ds(step * STEP * CELLS + high * 16 + q, STEP * 32, stride=32)
                spec[to, :] = got[:, high * 128 : (high + 1) * 128]

        @pl.loop(step * (STEP // GROUP), (step + 1) * (STEP // GROUP))
        def _(g):
            @pl.loop(0, GROUP, unroll=GROUP)
            def _(within):
                p = g * GROUP + within
                own = spec[pl.ds(pl.multiple_of(p * CELLS, CELLS), CELLS), :].astype(BF16)
                turned = dot(rot_ref[turn_ref[p]], own)
                factor = dot(left_ref[...], right_ref[:, pl.ds(pl.multiple_of(p * 128, 128), 128)])
                both = turned * factor
                at = within * CELLS
                wide[pl.ds(pl.multiple_of(at, CELLS), CELLS), :] = both + pltpu.roll(both, LANES // 2, 1)
                even = wide[pl.ds(at, CELLS // 2, stride=2), :]
                odd = wide[pl.ds(at + 1, CELLS // 2, stride=2), :]
                packed = jnp.where(first, even, odd).astype(BF16)
                send[:, p] = packed.reshape(owners, pairs, LANES)
                long = packed.astype(F32)
                energy_ref[pl.ds(p, 1), :] = jnp.sum(long * long, axis=0, keepdims=True)

            @pl.loop(1, owners)
            def _(k):
                data_copy(g, k).start()

    held[me] = send[me]

    @pl.loop(1, owners)
    def _(k):
        fact_copy(k).wait()

    load(CHUNKS + 5).wait()
    known = facts[...].reshape(particles, LANES)
    lane = lax.broadcasted_iota(jnp.int32, (particles, LANES), 1)
    member = jnp.where(known[:, 0:1] == lane.astype(F32), 1.0, 0.0)
    across = member.T[:class_count]
    defocus = known[:, 1:2]
    one = lax.broadcasted_iota(jnp.int32, (1, LANES), 1)
    kz = one % BAND - BAND // 2

    across = across.astype(BF16)
    quarter = lax.broadcasted_iota(jnp.int32, (class_count, LANES), 1) // BAND

    @pl.loop(0, pairs // 2, unroll=2)
    def _(r2):
        cell = (me * pairs + r2 * 2) * 2 + one // BAND
        kx = cell // BAND - BAND // 2
        ky = cell % BAND - BAND // 2
        radius = (kx * kx + ky * ky + kz * kz).astype(F32)
        weight = jnp.sin(defocus * radius / BAND + 0.3)
        high, low = halves(weight * weight)
        total = dot(across, high.astype(BF16)) + dot(across, low.astype(BF16))
        total = 1.0 / (total + 1.0)
        by_one, by_two, by_three = (pltpu.roll(total, i * BAND, 1) for i in (1, 2, 3))
        below[r2 * 2] = jnp.where(quarter == 0, total, jnp.where(quarter == 3, by_two, by_one))
        below[r2 * 2 + 1] = jnp.where(quarter == 3, total, jnp.where(quarter == 0, by_two, by_three))
        for i in range(2):
            r = r2 * 2 + i
            at = pl.ds(pl.multiple_of(r * LANES, LANES), LANES)
            chosen[r] = dot(member[:, :class_count].astype(BF16), refs_ref[:, at])

    @pl.loop(0, ROWS // GROUP)
    def _(g):
        @pl.loop(1, owners)
        def _(k):
            data_copy(g, k).wait()

    wide[0 : particles * pairs, :] = held[...].astype(F32).reshape(particles * pairs, LANES)
    parts[...] = jnp.zeros_like(parts)

    @pl.loop(0, pairs, unroll=4)
    def _(r):
        rows = wide[pl.ds(r, particles, stride=pairs), :]
        parts[...] += (rows * chosen[r]).reshape(owners, ROWS, LANES)

    @pl.loop(1, owners)
    def _(k):
        answer_copy(k).start()

    answer[me] = parts[me]

    @pl.loop(0, pairs, unroll=4)
    def _(r):
        rows = wide[pl.ds(r, particles, stride=pairs), :]
        total = dot(across, rows.astype(BF16))
        new_ref[:, pl.ds(pl.multiple_of(r * LANES, LANES), LANES)] = total * below[r]

    @pl.loop(1, owners)
    def _(k):
        answer_copy(k).wait()

    agreement = jnp.sum(jnp.sum(answer[...], axis=0), axis=1, keepdims=True)
    energy = jnp.sum(energy_ref[...], axis=1, keepdims=True)
    score_ref[...] = jnp.broadcast_to(agreement / jnp.sqrt(energy + 1e-06), (ROWS, LANES))


def on_device(owners, volumes, rotations, turn_ids, shifts, defocus, labels, references):
    class_count, columns = references.shape
    pairs = columns // LANES
    particles = owners * ROWS
    rows = volumes.reshape(ROWS, BOX, BOX * BOX).transpose(1, 0, 2).reshape(BOX * ROWS, BOX * BOX)
    constants = [jnp.asarray(t) for t in tables()]
    new_refs, scores = pl.pallas_call(
        lambda *refs: whole(owners, *refs),
        out_shape=(
            jax.ShapeDtypeStruct((class_count, columns), F32),
            jax.ShapeDtypeStruct((ROWS, LANES), F32),
        ),
        in_specs=[SMEM] * 4 + [HBM] * 7,
        out_specs=(VMEM, VMEM),
        scratch_shapes=[
            pltpu.VMEM(x.shape, BF16) for x in (rows, rotations, references, *constants)
        ] + [
            pltpu.VMEM((1024, 2048), BF16),
            pltpu.VMEM((512, 2048), BF16),
            pltpu.VMEM((16, 256, 256), BF16),
            pltpu.VMEM((ROWS * CELLS, LANES), F32),
            pltpu.VMEM((CELLS, LANES), BF16),
            pltpu.VMEM((LANES, ROWS * LANES), BF16),
            pltpu.VMEM((max(GROUP * CELLS, particles * pairs), LANES), F32),
            pltpu.VMEM((ROWS, LANES), F32),
            pltpu.VMEM((owners, ROWS, pairs, LANES), BF16),
            pltpu.VMEM((owners, ROWS, pairs, LANES), BF16),
            pltpu.VMEM((ROWS, LANES), F32),
            pltpu.VMEM((owners, ROWS, LANES), F32),
            pltpu.VMEM((pairs, particles, LANES), F32),
            pltpu.VMEM((pairs, class_count, LANES), F32),
            pltpu.VMEM((owners, ROWS, LANES), F32),
            pltpu.VMEM((owners, ROWS, LANES), F32),
            pltpu.SemaphoreType.DMA((CHUNKS + 6,)),
            pltpu.SemaphoreType.DMA((2, owners)),
            pltpu.SemaphoreType.DMA((ROWS // GROUP, 2, owners)),
            pltpu.SemaphoreType.DMA((2, owners)),
        ],
        compiler_params=pltpu.CompilerParams(
            collective_id=0, has_side_effects=True, vmem_limit_bytes=64 * 1024 * 1024
        ),
    )(turn_ids, labels, defocus, shifts.T, rows, rotations, references, *constants)
    return new_refs, scores[:, 0]


def solution(mesh):
    owners = mesh.shape["dev"]
    return jax.shard_map(
        lambda *args: on_device(owners, *args),
        mesh=mesh,
        in_specs=(
            P(("groups", "dev"), None),
            P(),
            P(("groups", "dev")),
            P(("groups", "dev"), None),
            P(("groups", "dev")),
            P(("groups", "dev")),
            P("groups", "dev"),
        ),
        out_specs=(P("groups", "dev"), P(("groups", "dev"))),
        check_vma=False,
    )
```

```python
import math

import jax
import jax.numpy as jnp
import ml_dtypes
import numpy as np
from jax import lax
from jax.experimental import pallas as pl
from jax.experimental.pallas import tpu as pltpu
from jax.sharding import PartitionSpec as P

BOX = 64
BAND = 32
ROWS = 8
CELLS = BAND * BAND
LANES = 128
CHUNKS = 8
GROUP = 2
STEPS = 4
STEP = ROWS // STEPS
TWO_PI = 2.0 * math.pi
VMEM = pl.BlockSpec(memory_space=pltpu.VMEM)
HBM = pl.BlockSpec(memory_space=pltpu.HBM)
SMEM = pl.BlockSpec(memory_space=pltpu.SMEM)
F32 = jnp.float32
BF16 = jnp.bfloat16


def rounded(table):
    table = np.asarray(table, np.float32).astype(ml_dtypes.bfloat16)
    return table.reshape(*table.shape[:-2], -1, 8, table.shape[-1])


def tables():
    n = np.arange(BOX)
    k = np.arange(BAND) - BAND // 2
    angle = TWO_PI * ((n[:, None] * k[None, :]) % BOX) / BOX
    cosine, sine = np.cos(angle) / 8.0, np.sin(angle) / 8.0
    by_z = np.zeros((4, 64, 2, 4, 32))
    for y in range(4):
        by_z[y, :, 0, y] = cosine
        by_z[y, :, 1, y] = -sine
    mixing = np.array([[cosine, sine], [-sine, cosine]])
    by_x = np.zeros((8, 2, 2, 16, 2, 64, 8))
    for p in range(8):
        by_x[p, :, :, :, :, :, p] = mixing.reshape(2, 2, 64, 2, 16).transpose(3, 0, 4, 1, 2)
    q = np.arange(16)
    turn = TWO_PI * ((q[:, None] * q[None, :]) % 16) / 16
    c, s = np.cos(turn) / 4.0, np.sin(turn) / 4.0
    by_h = np.zeros((16, 2, 16, 16, 2, 16))
    for low in range(16):
        by_h[:, 0, low, :, 0, low] = c
        by_h[:, 0, low, :, 1, low] = s
        by_h[:, 1, low, :, 0, low] = -s
        by_h[:, 1, low, :, 1, low] = c
    by_y = np.zeros((16, 2, 4, 32, 2, 2, 2, 32))
    for high in range(2):
        for y in range(4):
            part = TWO_PI * (((high * 16 + q - 16) * y) % 64) / 64
            c, s = (np.cos(part) / 2.0)[:, None], (np.sin(part) / 2.0)[:, None]
            z = np.arange(32)
            by_y[:, 0, y, z, high, 0, 0, z] = c
            by_y[:, 1, y, z, high, 0, 0, z] = s
            by_y[:, 0, y, z, high, 0, 1, z] = -s
            by_y[:, 1, y, z, high, 0, 1, z] = c
            by_y[:, 0, y, z, high, 1, 0, z] = s
            by_y[:, 1, y, z, high, 1, 0, z] = -c
            by_y[:, 0, y, z, high, 1, 1, z] = c
            by_y[:, 1, y, z, high, 1, 1, z] = s
    return (
        rounded(by_z.reshape(256, 256)),
        rounded(by_x.reshape(512, 1024)),
        rounded(by_h.reshape(512, 512)),
        rounded(by_y.reshape(16, 256, 256)),
    )


def dot(a, b):
    return jnp.dot(a, b, preferred_element_type=F32)


def root(count):
    angle = (count - 64.0 * jnp.floor(count / 64.0)) * (TWO_PI / 64.0)
    return jnp.cos(angle), jnp.sin(angle)


def halves(x):
    high = x.astype(BF16).astype(F32)
    return high, x - high


def factors(facts):
    defocus, sx, sy, sz = (facts[:, i : i + 1] for i in range(1, 5))
    cell = lax.broadcasted_iota(jnp.int32, (ROWS, CELLS), 1)
    kx = (cell // BAND - BAND // 2).astype(F32)
    ky = (cell % BAND - BAND // 2).astype(F32)
    focus = defocus * (kx * kx + ky * ky) / BAND + 0.3
    cos_a, sin_a = root(kx * sx + ky * sy)
    cos_f, sin_f = jnp.cos(focus), jnp.sin(focus)
    rows = [halves(x) for x in (sin_f * cos_a, sin_f * sin_a, cos_f * cos_a, cos_f * sin_a)]
    lane = lax.broadcasted_iota(jnp.int32, (ROWS, LANES), 1)
    kz = (lane % BAND - BAND // 2).astype(F32)
    cos_b, sin_b = root(kz * sz)
    first = lane < LANES // 2
    one = jnp.where(first, cos_b, sin_b)
    two = jnp.where(first, -sin_b, cos_b)
    focus = defocus * (kz * kz) / BAND
    cos_f, sin_f = jnp.cos(focus), jnp.sin(focus)
    lanes = [halves(x) for x in (cos_f * one, cos_f * two, sin_f * one, sin_f * two)]
    blank = jnp.zeros((32, CELLS), F32)
    left = jnp.concatenate(
        [r[0] for r in rows] + [r[0] for r in rows] + [r[1] for r in rows] + [blank], axis=0
    )
    right = jnp.concatenate(
        [x[0] for x in lanes] + [x[1] for x in lanes] + [x[0] for x in lanes] + [blank[:, :LANES]], axis=0
    )
    owner = lax.broadcasted_iota(jnp.int32, (LANES, LANES), 0) % ROWS
    right = [jnp.where(owner == p, right, 0.0) for p in range(ROWS)]
    return left.T.astype(BF16), jnp.concatenate(right, axis=1).astype(BF16)


def collect(labels, defocus, shifts):
    row = lax.broadcasted_iota(jnp.int32, (ROWS, LANES), 0)
    lane = lax.broadcasted_iota(jnp.int32, (ROWS, LANES), 1)
    facts = jnp.zeros((ROWS, LANES), F32)
    for p in range(ROWS):
        values = [labels[p].astype(F32), defocus[p]] + [shifts[i, p].astype(F32) for i in range(3)]
        for i, value in enumerate(values):
            facts = jnp.where((row == p) & (lane == i), value, facts)
    return facts


def whole(owners, turn_ref, label_ref, defocus_ref, shift_ref, vol_hbm, rot_hbm, refs_hbm,
          z_hbm, x_hbm, h_hbm, y_hbm, new_ref, score_ref,
          vol_ref, rot_ref, refs_ref, z_ref, x_ref, h_ref, y_ref,
          by_z, by_x, by_h, spec, left_ref, right_ref, wide, energy_ref,
          send, held, facts_ref, facts, chosen, below, parts, answer, load_sems, fact_sems, data_sems, answer_sems):
    me = lax.axis_index("dev")
    class_count, columns = refs_ref.shape
    pairs = columns // LANES
    particles = owners * ROWS

    def load(i):
        if i < CHUNKS:
            at = pl.ds(i * (4096 // CHUNKS), 4096 // CHUNKS)
            src, dst = vol_hbm.at[:, at], vol_ref.at[:, at]
        else:
            src, dst = (
                (z_hbm, z_ref), (x_hbm, x_ref), (h_hbm, h_ref), (y_hbm, y_ref), (rot_hbm, rot_ref), (refs_hbm, refs_ref)
            )[i - CHUNKS]
        return pltpu.make_async_copy(src, dst, load_sems.at[i])

    for i in (CHUNKS, *range(CHUNKS), *range(CHUNKS + 1, CHUNKS + 6)):
        load(i).start()

    def remote(src, dst, sems, to, k):
        return pltpu.make_async_remote_copy(
            src_ref=src, dst_ref=dst, send_sem=sems.at[0, k], recv_sem=sems.at[1, k],
            device_id={"dev": to}, device_id_type=pl.DeviceIdType.MESH,
        )

    def fact_copy(k):
        return remote(facts_ref, facts.at[me], fact_sems, lax.rem(me + k, owners), k)

    def data_copy(g, k):
        to = lax.rem(me + k, owners)
        at = pl.ds(g * GROUP, GROUP)
        return remote(send.at[to, at], held.at[me, at], data_sems.at[g], to, k)

    def answer_copy(k):
        to = lax.rem(me + k, owners)
        return remote(parts.at[to], answer.at[me], answer_sems, to, k)

    barrier = pltpu.get_barrier_semaphore()

    @pl.loop(1, owners)
    def _(k):
        pl.semaphore_signal(
            barrier, inc=1, device_id={"dev": lax.rem(me + k, owners)}, device_id_type=pl.DeviceIdType.MESH
        )

    own_facts = collect(label_ref, defocus_ref, shift_ref)
    facts_ref[...] = own_facts
    left, right = factors(own_facts)
    left_ref[...] = left
    right_ref[...] = right

    load(CHUNKS).wait()
    for chunk in range(CHUNKS):
        load(chunk).wait()

        @pl.loop(chunk * (16 // CHUNKS), (chunk + 1) * (16 // CHUNKS), unroll=2)
        def _(h):
            got = dot(vol_ref[:, pl.ds(pl.multiple_of(h * 256, 256), 256)], z_ref[...].reshape(256, 256)).astype(BF16)
            at = pl.ds(pl.multiple_of(h * 128, 128), 128)
            by_z[0:512, at] = got[:, :128]
            by_z[512:1024, at] = got[:, 128:]

    load(CHUNKS + 1).wait()

    @pl.loop(0, 8, unroll=4)
    def _(h2):
        got = dot(x_ref[...].reshape(512, 1024), by_z[:, pl.ds(pl.multiple_of(h2 * 256, 256), 256)]).astype(BF16)
        for i in range(2):
            to = pl.ds(pl.multiple_of(h2 * 64 + i * 32, 32), 32)
            for g in range(16):
                by_x[to, g * 128 : (g + 1) * 128] = got[g * 32 : (g + 1) * 32, i * 128 : (i + 1) * 128]

    pl.semaphore_wait(barrier, owners - 1)

    @pl.loop(1, owners)
    def _(k):
        fact_copy(k).start()

    facts[me] = facts_ref[...]
    first = lax.broadcasted_iota(jnp.int32, (CELLS // 2, LANES), 1) < LANES // 2
    for i in (2, 3, 4):
        load(CHUNKS + i).wait()

    @pl.loop(0, STEPS)
    def _(step):
        @pl.loop(0, STEP, unroll=min(STEP, 2))
        def _(within):
            p = step * STEP + within
            got = dot(h_ref[...].reshape(512, 512), by_x[:, pl.ds(pl.multiple_of(p * 256, 256), 256)]).astype(BF16)
            got = got.reshape(16, 2, 16, 256)
            for i in range(2):
                to = pl.ds(pl.multiple_of(p * 32 + i * 16, 16), 16)
                for c in range(2):
                    by_h[:, to, c * 128 : (c + 1) * 128] = got[:, c, :, i * 128 : (i + 1) * 128]

        @pl.loop(0, 16, unroll=8)
        def _(q):
            own = by_h[q, pl.ds(pl.multiple_of(step * STEP * 32, STEP * 32), STEP * 32), :]
            got = dot(own, y_ref[q].reshape(256, 256))
            for high in range(2):
                to = pl.ds(step * STEP * CELLS + high * 16 + q, STEP * 32, stride=32)
                spec[to, :] = got[:, high * 128 : (high + 1) * 128]

        @pl.loop(step * (STEP // GROUP), (step + 1) * (STEP // GROUP))
        def _(g):
            @pl.loop(0, GROUP, unroll=GROUP)
            def _(within):
                p = g * GROUP + within
                own = spec[pl.ds(pl.multiple_of(p * CELLS, CELLS), CELLS), :].astype(BF16)
                turned = dot(rot_ref[turn_ref[p]], own)
                factor = dot(left_ref[...], right_ref[:, pl.ds(pl.multiple_of(p * 128, 128), 128)])
                both = turned * factor
                at = within * CELLS
                wide[pl.ds(pl.multiple_of(at, CELLS), CELLS), :] = both + pltpu.roll(both, LANES // 2, 1)
                even = wide[pl.ds(at, CELLS // 2, stride=2), :]
                odd = wide[pl.ds(at + 1, CELLS // 2, stride=2), :]
                packed = jnp.where(first, even, odd).astype(BF16)
                send[:, p] = packed.reshape(owners, pairs, LANES)
                long = packed.astype(F32)
                energy_ref[pl.ds(p, 1), :] = jnp.sum(long * long, axis=0, keepdims=True)

            @pl.loop(1, owners)
            def _(k):
                data_copy(g, k).start()

    held[me] = send[me]

    @pl.loop(1, owners)
    def _(k):
        fact_copy(k).wait()

    load(CHUNKS + 5).wait()
    known = facts[...].reshape(particles, LANES)
    lane = lax.broadcasted_iota(jnp.int32, (particles, LANES), 1)
    member = jnp.where(known[:, 0:1] == lane.astype(F32), 1.0, 0.0)
    across = member.T[:class_count]
    defocus = known[:, 1:2]
    one = lax.broadcasted_iota(jnp.int32, (1, LANES), 1)
    kz = one % BAND - BAND // 2

    across = across.astype(BF16)
    quarter = lax.broadcasted_iota(jnp.int32, (class_count, LANES), 1) // BAND

    @pl.loop(0, pairs // 2, unroll=2)
    def _(r2):
        cell = (me * pairs + r2 * 2) * 2 + one // BAND
        kx = cell // BAND - BAND // 2
        ky = cell % BAND - BAND // 2
        radius = (kx * kx + ky * ky + kz * kz).astype(F32)
        weight = jnp.sin(defocus * radius / BAND + 0.3)
        high, low = halves(weight * weight)
        total = dot(across, high.astype(BF16)) + dot(across, low.astype(BF16))
        total = 1.0 / (total + 1.0)
        by_one, by_two, by_three = (pltpu.roll(total, i * BAND, 1) for i in (1, 2, 3))
        below[r2 * 2] = jnp.where(quarter == 0, total, jnp.where(quarter == 3, by_two, by_one))
        below[r2 * 2 + 1] = jnp.where(quarter == 3, total, jnp.where(quarter == 0, by_two, by_three))
        for i in range(2):
            r = r2 * 2 + i
            at = pl.ds(pl.multiple_of(r * LANES, LANES), LANES)
            chosen[r] = dot(member[:, :class_count].astype(BF16), refs_ref[:, at])

    @pl.loop(0, ROWS // GROUP)
    def _(g):
        @pl.loop(1, owners)
        def _(k):
            data_copy(g, k).wait()

    wide[0 : particles * pairs, :] = held[...].astype(F32).reshape(particles * pairs, LANES)
    parts[...] = jnp.zeros_like(parts)

    @pl.loop(0, pairs, unroll=4)
    def _(r):
        rows = wide[pl.ds(r, particles, stride=pairs), :]
        parts[...] += (rows * chosen[r]).reshape(owners, ROWS, LANES)

    @pl.loop(1, owners)
    def _(k):
        answer_copy(k).start()

    answer[me] = parts[me]

    @pl.loop(0, pairs, unroll=4)
    def _(r):
        rows = wide[pl.ds(r, particles, stride=pairs), :]
        total = dot(across, rows.astype(BF16))
        new_ref[:, pl.ds(pl.multiple_of(r * LANES, LANES), LANES)] = total * below[r]

    @pl.loop(1, owners)
    def _(k):
        answer_copy(k).wait()

    agreement = jnp.sum(jnp.sum(answer[...], axis=0), axis=1, keepdims=True)
    energy = jnp.sum(energy_ref[...], axis=1, keepdims=True)
    score = jnp.broadcast_to(agreement / jnp.sqrt(energy + 1e-06), (ROWS, LANES))
    score_ref[...] = score.T[0:1]


def on_device(owners, volumes, rotations, turn_ids, shifts, defocus, labels, references):
    class_count, columns = references.shape
    pairs = columns // LANES
    particles = owners * ROWS
    rows = volumes.reshape(ROWS, BOX, BOX * BOX).transpose(1, 0, 2).reshape(BOX * ROWS, BOX * BOX)
    constants = [jnp.asarray(t) for t in tables()]
    new_refs, scores = pl.pallas_call(
        lambda *refs: whole(owners, *refs),
        out_shape=(
            jax.ShapeDtypeStruct((class_count, columns), F32),
            jax.ShapeDtypeStruct((1, ROWS), F32),
        ),
        in_specs=[SMEM] * 4 + [HBM] * 7,
        out_specs=(VMEM, VMEM),
        scratch_shapes=[
            pltpu.VMEM(x.shape, BF16) for x in (rows, rotations, references, *constants)
        ] + [
            pltpu.VMEM((1024, 2048), BF16),
            pltpu.VMEM((512, 2048), BF16),
            pltpu.VMEM((16, 256, 256), BF16),
            pltpu.VMEM((ROWS * CELLS, LANES), F32),
            pltpu.VMEM((CELLS, LANES), BF16),
            pltpu.VMEM((LANES, ROWS * LANES), BF16),
            pltpu.VMEM((max(GROUP * CELLS, particles * pairs), LANES), F32),
            pltpu.VMEM((ROWS, LANES), F32),
            pltpu.VMEM((owners, ROWS, pairs, LANES), BF16),
            pltpu.VMEM((owners, ROWS, pairs, LANES), BF16),
            pltpu.VMEM((ROWS, LANES), F32),
            pltpu.VMEM((owners, ROWS, LANES), F32),
            pltpu.VMEM((pairs, particles, LANES), F32),
            pltpu.VMEM((pairs, class_count, LANES), F32),
            pltpu.VMEM((owners, ROWS, LANES), F32),
            pltpu.VMEM((owners, ROWS, LANES), F32),
            pltpu.SemaphoreType.DMA((CHUNKS + 6,)),
            pltpu.SemaphoreType.DMA((2, owners)),
            pltpu.SemaphoreType.DMA((ROWS // GROUP, 2, owners)),
            pltpu.SemaphoreType.DMA((2, owners)),
        ],
        compiler_params=pltpu.CompilerParams(
            collective_id=0, has_side_effects=True, vmem_limit_bytes=64 * 1024 * 1024
        ),
    )(turn_ids, labels, defocus, shifts.T, rows, rotations, references, *constants)
    return new_refs, scores[0]


def solution(mesh):
    owners = mesh.shape["dev"]
    return jax.shard_map(
        lambda *args: on_device(owners, *args),
        mesh=mesh,
        in_specs=(
            P(("groups", "dev"), None),
            P(),
            P(("groups", "dev")),
            P(("groups", "dev"), None),
            P(("groups", "dev")),
            P(("groups", "dev")),
            P("groups", "dev"),
        ),
        out_specs=(P("groups", "dev"), P(("groups", "dev"))),
        check_vma=False,
    )
```
